256 devices in a mesh: grp: 8 (over z_lo, core), row: 4 (over y), col: 8 (over z_hi, x).
Axes of the slice: x: 4, y: 4, z: 8 (z_hi: 2, z_lo: 4; z = z_hi * 4 + z_lo), core: 2. Of those that a mesh axis runs over, the one named last changes fastest.
Arguments:
- top_covariance: bfloat16 [12288, 1536], P(('grp', 'row', 'col')), parts along dimension 0, as said below
- first_panel: bfloat16 [256, 8, 128, 128], P(('grp', 'row', 'col')), parts along dimension 0, may hold values from -0.1796875 to 0.1796875
- first_inverse: bfloat16 [256, 128, 128], P(('grp', 'row', 'col')), parts along dimension 0, as said below
- first_index: int32 [256, 8], P(('grp', 'row', 'col')), parts along dimension 0, may hold values from 0 to 11, as said below
- second_panel: bfloat16 [8192, 4, 128, 128], P(('grp', 'row', 'col')), parts along dimension 0, may hold values from -0.1796875 to 0.1796875
- second_inverse: bfloat16 [8192, 128, 128], P(('grp', 'row', 'col')), parts along dimension 0, as said below
- second_positions: int32 [8192, 3], P(('grp', 'row', 'col')), parts along dimension 0, may hold values from 0 to 7, as said below
- row_order: int32 [1048576], P(('grp', 'row', 'col')), parts along dimension 0, may hold values from 0 to 4095, as said below
- sensitivity: bfloat16 [256, 256, 128], P(('grp', 'row', 'col')), parts along dimension 0, may hold values from -0.375 to 0.375
Outputs:
- first_cross: bfloat16 [256, 8, 128, 128], P(('grp', 'row', 'col')), parts along dimension 0
- first_diag: bfloat16 [256, 128, 128], P(('grp', 'row', 'col')), parts along dimension 0
- second_cross: bfloat16 [8192, 4, 128, 128], P(('grp', 'row', 'col')), parts along dimension 0
- second_diag: bfloat16 [8192, 128, 128], P(('grp', 'row', 'col')), parts along dimension 0
- tile_products: bfloat16 [1048576, 128], P(('grp', 'row', 'col')), parts along dimension 0
The draws below stay inside these ranges and needn't reach their ends.
There are 8 independent parts, one for each index of `grp`. The reference program is written for one: setup_inputs(seed, part) draws one part's arguments, and reference() takes and returns one part's arrays. A program takes and returns all parts, laid end to end along the dimension named above; each array names one. Nothing has to cross between parts.
Inputs may be any that keep to these rules, and one draw needn't show every extreme that they name: `first_index`: each row holds 8 distinct block numbers in increasing order. `second_positions`: each row holds 3 distinct positions in increasing order. `row_order`: for every t, entries t * 32 * 128 to (t + 1) * 32 * 128 - 1 are a permutation of 0 to 4095. `top_covariance`: symmetric and positive definite. `first_inverse`: lower triangular with a diagonal of 0.8 to 1.25. `second_inverse`: lower triangular with a diagonal of 0.8 to 1.25.
All inputs are finite; a program needn't handle non-finite values.
Results may differ from the reference program's by a relative error of at most 0.006.
Values may be sent and summed in bfloat16 or wider, within the bound.
No kernel may reach another device: no remote copies, remote signals or barrier semaphores. Data moves between devices by JAX's collectives and lax.ppermute only.
A program may use at most 192 MiB of HBM per device.

```python
import math
import jax
import jax.numpy as jnp
from jax import lax

B = 128
NA = 12
P_SIZE = 8
Q = 3
CH = 32
NH = 128
TILES = 32
K1 = 32
K2 = 1024
PIECE = 128


def triangle_draw(key, count):
    key_noise, key_diag = jax.random.split(key, 2)
    rows = lax.broadcasted_iota(jnp.int32, (count, B, B), 1)
    cols = lax.broadcasted_iota(jnp.int32, (count, B, B), 2)
    noise = jax.random.normal(key_noise, (count, B, B), jnp.float32)
    diag_vals = jax.random.uniform(key_diag, (count, B, B), jnp.float32, 0.8, 1.25)
    lower = jnp.where(rows > cols, noise * (0.5 / math.sqrt(B)), 0.0)
    result = lower + jnp.where(rows == cols, diag_vals, 0.0)
    return result.astype(jnp.bfloat16)


def draw_first_inverse(key, part):
    return triangle_draw(jax.random.fold_in(key, 11), K1)


def draw_second_inverse(key, part):
    return triangle_draw(jax.random.fold_in(key, 12), K2)


def draw_top_covariance(key, part):
    total = NA * B
    key_a, key_b = jax.random.split(jax.random.fold_in(key, 13), 2)
    raw = jax.random.normal(key_a, (total, total), jnp.float32)
    sym = (raw + raw.T) * (0.28 / math.sqrt(total))
    rows = lax.broadcasted_iota(jnp.int32, (total, total), 0)
    cols = lax.broadcasted_iota(jnp.int32, (total, total), 1)
    diag_vals = jax.random.uniform(key_b, (total,), jnp.float32, 1.0, 2.0)
    matrix = sym + jnp.where(rows == cols, diag_vals[:, None], 0.0)
    return matrix.astype(jnp.bfloat16)


def choose_sorted(key, count, among, keep):
    keys = jax.random.split(key, count)
    return jax.vmap(lambda one_key: jnp.sort(jax.random.permutation(one_key, among)[:keep]))(keys).astype(jnp.int32)


def draw_first_index(key, part):
    return choose_sorted(jax.random.fold_in(key, 14), K1, NA, P_SIZE)


def draw_second_positions(key, part):
    return choose_sorted(jax.random.fold_in(key, 15), K2, P_SIZE, Q)


def draw_row_order(key, part):
    keys = jax.random.split(jax.random.fold_in(key, 16), TILES)
    orders = jax.vmap(lambda one_key: jax.random.permutation(one_key, CH * B))(keys)
    return orders.reshape(K2 * B).astype(jnp.int32)


def shard_levels(key, shape, cuts, low, top_value):
    factor_of = 1.0
    for position, blocks in cuts:
        steps = jax.random.uniform(jax.random.fold_in(jax.random.fold_in(key, 6), position), (blocks,), jnp.float32, low / len(cuts), top_value / len(cuts))
        factor_of = factor_of * jnp.repeat(jnp.exp(steps), shape[position] // blocks).reshape((-1,) + (1,) * (len(shape) - 1 - position))
    return factor_of


def centred(own_key, shape, width, limit, cuts=(), kind=jnp.bfloat16):
    entries = jax.random.normal(own_key, shape, jnp.float32) * width
    if len(cuts) > 0:
        entries = shard_levels(own_key, shape, cuts, -0.22, 0.18) * entries
    return jnp.clip(entries, min=-limit, max=limit).astype(kind)


def setup_inputs(seed: int = 0, part: int = 0) -> dict:
    key_of = jax.random.split(jax.random.key(seed), 10)
    part_splits = jax.random.split(jax.random.fold_in(key_of[9], part), 10)
    top_covariance = draw_top_covariance(jax.random.fold_in(jax.random.fold_in(key_of[9], part), 71), part)
    first_panel = centred(part_splits[1], (K1, P_SIZE, B, B), 0.03, 0.1796875, ((0, 32),))
    first_inverse = draw_first_inverse(jax.random.fold_in(jax.random.fold_in(key_of[9], part), 71), part)
    first_index = draw_first_index(jax.random.fold_in(jax.random.fold_in(key_of[9], part), 71), part)
    second_panel = centred(part_splits[4], (K2, Q + 1, B, B), 0.03, 0.1796875, ((0, 32),))
    second_inverse = draw_second_inverse(jax.random.fold_in(jax.random.fold_in(key_of[9], part), 71), part)
    second_positions = draw_second_positions(jax.random.fold_in(jax.random.fold_in(key_of[9], part), 71), part)
    row_order = draw_row_order(jax.random.fold_in(jax.random.fold_in(key_of[9], part), 71), part)
    sensitivity = centred(part_splits[8], (TILES, 2 * B, NH), (2 * B) ** -0.5, 0.375, ((0, 32),))
    return dict(top_covariance=top_covariance, first_panel=first_panel, first_inverse=first_inverse, first_index=first_index, second_panel=second_panel, second_inverse=second_inverse, second_positions=second_positions, row_order=row_order, sensitivity=sensitivity)


def supernode(top_blocks, packed):
    panel_one, inverse_one, index_one, panel_two, inverse_two, positions = packed
    first_u = jnp.einsum('pxy,yz->pxz', panel_one.astype(jnp.float32), inverse_one.astype(jnp.float32)).astype(jnp.bfloat16)
    second_u = jnp.einsum('ckxy,cyz->ckxz', panel_two.astype(jnp.float32), inverse_two.astype(jnp.float32)).astype(jnp.bfloat16)
    sub_top = jnp.take(jnp.take(top_blocks, index_one, axis=0), index_one, axis=2)
    front_first = jnp.einsum('pxqy,qyz->pxz', sub_top.astype(jnp.float32), first_u.astype(jnp.float32))
    child_sub = jax.vmap(lambda pos_row: jnp.take(jnp.take(sub_top, pos_row, axis=0), pos_row, axis=2))(positions)
    front_second = jnp.einsum('crxqy,cqyz->crxz', child_sub.astype(jnp.float32), second_u[:, 1:].astype(jnp.float32))
    first_cross = (-front_first).astype(jnp.bfloat16)
    inverse_f = inverse_one.astype(jnp.float32)
    first_diag = (jnp.einsum('yx,yz->xz', inverse_f, inverse_f)
                  - jnp.einsum('pyx,pyz->xz', first_u.astype(jnp.float32), first_cross.astype(jnp.float32))).astype(jnp.bfloat16)
    picked = jnp.take(first_cross, positions, axis=0).astype(jnp.float32)
    parent_u = second_u[:, 0].astype(jnp.float32)
    rest_u = second_u[:, 1:].astype(jnp.float32)
    cross_zero = -(jnp.einsum('xy,cyz->cxz', first_diag.astype(jnp.float32), parent_u)
                   + jnp.einsum('cqyx,cqyz->cxz', picked, rest_u))
    cross_rest = -(jnp.einsum('cqxy,cyz->cqxz', picked, parent_u) + front_second)
    second_cross = jnp.concatenate([cross_zero[:, None], cross_rest], axis=1).astype(jnp.bfloat16)
    inverse_two_f = inverse_two.astype(jnp.float32)
    second_diag = (jnp.einsum('cyx,cyz->cxz', inverse_two_f, inverse_two_f)
                   - jnp.einsum('ckyx,ckyz->cxz', second_u.astype(jnp.float32), second_cross.astype(jnp.float32))).astype(jnp.bfloat16)
    return first_cross, first_diag, second_cross, second_diag


def reference(top_covariance, first_panel, first_inverse, first_index, second_panel, second_inverse, second_positions, row_order, sensitivity):
    top_blocks = top_covariance.reshape(NA, B, NA, B)
    packed = (first_panel, first_inverse, first_index,
              second_panel.reshape(K1, CH, Q + 1, B, B),
              second_inverse.reshape(K1, CH, B, B),
              second_positions.reshape(K1, CH, Q))
    first_cross, first_diag, second_cross, second_diag = lax.map(lambda item: supernode(top_blocks, item), packed)
    second_cross = second_cross.reshape(K2, Q + 1, B, B)
    second_diag = second_diag.reshape(K2, B, B)
    cov_rows = jnp.concatenate([second_diag, second_cross[:, 0]], axis=-1).reshape(K2 * B, 2 * B)
    out_index = jnp.arange(K2 * B, dtype=jnp.int32)
    tile_index = out_index // (CH * B)
    within = out_index % (CH * B)
    source = within // PIECE
    offset = within % PIECE
    lookup = (source * (CH * B) + tile_index * PIECE + offset).astype(jnp.int32)
    source_rows = (source * (CH * B) + jnp.take(row_order, lookup, axis=0)).astype(jnp.int32)
    relaid = jnp.take(cov_rows, source_rows, axis=0).reshape(TILES, CH * B, 2 * B)
    tile_products = jnp.einsum('tmb,tbh->tmh', relaid.astype(jnp.float32), sensitivity.astype(jnp.float32)).astype(jnp.bfloat16)
    return first_cross, first_diag, second_cross, second_diag, tile_products.reshape(K2 * B, NH)
```

```python
import functools

import jax
import jax.numpy as jnp
from jax import lax
from jax.experimental import pallas as pl
from jax.experimental.pallas import tpu as pltpu
from jax.sharding import PartitionSpec as P

B = 128
NA = 12
PS = 8
Q = 3
WIN = 8
SHARD = 48
F32 = jnp.float32
BF = jnp.bfloat16
REL = (0, 1, -1, 2)


def mm(a, b):
    return jnp.dot(a, b, preferred_element_type=F32)


def mm_tn(a, b):
    return lax.dot_general(a, b, (((0,), (0,)), ((), ())), preferred_element_type=F32)


def mm_tt(a, b):
    return lax.dot_general(a, b, (((0,), (1,)), ((), ())), preferred_element_type=F32)


def flip(x):
    return x.astype(F32).T.astype(BF)


def pack_kernel(pos, x_ref, o_ref):
    first = (3 * pos[0]) // 8
    for k in range(WIN):
        col = lax.rem(first + k, NA)
        o_ref[k // 4, k % 4] = x_ref[:, pl.ds(pl.multiple_of(col * B, B), B)]


def pack(x, me):
    return pl.pallas_call(
        pack_kernel,
        out_shape=jax.ShapeDtypeStruct((2, 4, SHARD, B), BF),
        in_specs=[
            pl.BlockSpec(memory_space=pltpu.SMEM),
            pl.BlockSpec(memory_space=pltpu.VMEM),
        ],
        out_specs=pl.BlockSpec(memory_space=pltpu.VMEM),
        name="pack",
    )(me.reshape(1), x)


KIDS = 4


def early_kernel(fp, fi, sp, si, fu, fut, fw, su, sut, sw):
    @pl.when(pl.program_id(0) == 0)
    def _():
        inv = fi[0]
        pan = fp[0].reshape(PS * B, B)
        fu[...] = mm(pan, inv).astype(BF)
        fut[...] = mm_tt(inv, pan).astype(BF)
        fw[...] = mm_tn(inv, inv)

    for c in range(KIDS):
        inv = si[c]
        pan = sp[c].reshape((Q + 1) * B, B)
        su[c] = mm(pan, inv).astype(BF)
        sut[c] = mm_tt(inv, pan).astype(BF)
        sw[c] = mm_tn(inv, inv)


def early(fp, fi, sp, si):
    n = sp.shape[0]
    whole = lambda *s: pl.BlockSpec(s, lambda i: (0,) * len(s))
    part = lambda *s: pl.BlockSpec((KIDS,) + s, lambda i: (i,) + (0,) * len(s))
    return pl.pallas_call(
        early_kernel,
        grid=(n // KIDS,),
        out_shape=(
            jax.ShapeDtypeStruct((PS * B, B), BF),
            jax.ShapeDtypeStruct((B, PS * B), BF),
            jax.ShapeDtypeStruct((B, B), F32),
            jax.ShapeDtypeStruct((n, (Q + 1) * B, B), BF),
            jax.ShapeDtypeStruct((n, B, (Q + 1) * B), BF),
            jax.ShapeDtypeStruct((n, B, B), F32),
        ),
        in_specs=[
            whole(1, PS, B, B),
            whole(1, B, B),
            part(Q + 1, B, B),
            part(B, B),
        ],
        out_specs=(
            whole(PS * B, B),
            whole(B, PS * B),
            whole(B, B),
            part((Q + 1) * B, B),
            part(B, (Q + 1) * B),
            part(B, B),
        ),
        cost_estimate=pl.CostEstimate(
            flops=300 * 2 * B**3, bytes_accessed=20 * 2**20, transcendentals=0
        ),
        compiler_params=pltpu.CompilerParams(vmem_limit_bytes=32 * 2**20),
        name="early",
    )(fp, fi, sp, si)


def late_kernel(
    steps, pos, fidx, spos, order,
    a0, a1, a2, a3, b0, b1, b2, b3, fu, fut, fw, su, sut, sw,
    fc_o, fd_o, sc_o, sd_o, rows_o,
    full, tmat, cov, got,
):
    step = pl.program_id(0)

    @pl.when(step == 0)
    def _():
        me = pos[0]
        row, zh, x = me // 8, (me // 4) % 2, me % 4
        for half, group in enumerate(((a0, a1, a2, a3), (b0, b1, b2, b3))):
            for t in range(4):
                for u in range(4):
                    dr, dx = (REL[t], REL[u]) if half == 0 else (REL[u], REL[t])
                    r = lax.rem(row - dr + 4, 4)
                    xx = lax.rem(x - dx + 4, 4)
                    for z in range(2):
                        src = r * 8 + lax.rem(zh + z, 2) * 4 + xx
                        first = (3 * src) // 8
                        at = pl.multiple_of(src * SHARD, 16)
                        for k in range(4):
                            col = lax.rem(first + half * 4 + k, NA)
                            full[pl.ds(at, SHARD), pl.ds(pl.multiple_of(col * B, B), B)] = (
                                group[t][u, z, k]
                            )

        def block(p, q):
            return full[
                pl.ds(pl.multiple_of(p * B, B), B), pl.ds(pl.multiple_of(q * B, B), B)
            ]

        for p in range(PS):
            ap = fidx[0, p]
            tmat[(1 + p) * B:(2 + p) * B, (1 + p) * B:(2 + p) * B] = block(ap, ap)
            for q in range(p + 1, PS):
                aq = fidx[0, q]
                near = aq - ap <= 6
                i, j = jnp.where(near, p, q), jnp.where(near, q, p)
                held = block(jnp.where(near, ap, aq), jnp.where(near, aq, ap))
                ri = pl.ds(pl.multiple_of((1 + i) * B, B), B)
                rj = pl.ds(pl.multiple_of((1 + j) * B, B), B)
                tmat[ri, rj] = held
                tmat[rj, ri] = flip(held)
        cross = (-mm(tmat[B:, B:], fu[...])).astype(BF)
        fc_o[...] = cross.reshape(1, PS, B, B)
        tmat[B:, :B] = cross
        for p in range(PS):
            tmat[:B, (1 + p) * B:(2 + p) * B] = flip(cross[p * B:(p + 1) * B])
        diag = (fw[...] - mm(fut[...], cross)).astype(BF)
        fd_o[0] = diag
        tmat[:B, :B] = diag

    @pl.when(step < steps)
    def _():
        for c in range(KIDS):
            kid = step * KIDS + c
            at = [0] + [(1 + spos[kid * Q + q]) * B for q in range(Q)]
            at = [pl.ds(pl.multiple_of(v, B), B) for v in at]
            u = su[c]
            ws = []
            for r in range(Q + 1):
                line = jnp.concatenate([tmat[at[r], at[q]] for q in range(Q + 1)], axis=1)
                w = (-mm(line, u)).astype(BF)
                sc_o[c, r] = w
                ws.append(w)
            d = (sw[c] - mm(sut[c], jnp.concatenate(ws, axis=0))).astype(BF)
            sd_o[c] = d
            base = kid * 2 * B
            cov[pl.ds(base, B, stride=2), :] = d.astype(F32)
            cov[pl.ds(base + 1, B, stride=2), :] = ws[0].astype(F32)

    @pl.when(step >= steps)
    def _():
        n = KIDS * B
        base = (step - steps) * n

        def body(g, carry):
            for j in range(16):
                src = order[base + g * 16 + j]
                got[pl.ds(pl.multiple_of(g * 32, 32) + 2 * j, 2), :] = cov[
                    pl.ds(pl.multiple_of(src * 2, 2), 2), :
                ]
            return carry

        lax.fori_loop(0, n // 16, body, 0)
        rows_o[:, :B] = got[pl.ds(0, n, stride=2), :].astype(BF)
        rows_o[:, B:] = got[pl.ds(1, n, stride=2), :].astype(BF)


def late(me, fidx, spos, order, ga, gb, fu, fut, fw, su, sut, sw):
    n = su.shape[0]
    steps = n // KIDS
    whole = lambda *s: pl.BlockSpec(s, lambda i: (0,) * len(s))
    part = lambda *s: pl.BlockSpec(
        (KIDS,) + s, lambda i: (jnp.minimum(i, steps - 1),) + (0,) * len(s)
    )
    smem = pl.BlockSpec(memory_space=pltpu.SMEM)
    return pl.pallas_call(
        functools.partial(late_kernel, steps),
        grid=(2 * steps,),
        out_shape=(
            jax.ShapeDtypeStruct((1, PS, B, B), BF),
            jax.ShapeDtypeStruct((1, B, B), BF),
            jax.ShapeDtypeStruct((n, Q + 1, B, B), BF),
            jax.ShapeDtypeStruct((n, B, B), BF),
            jax.ShapeDtypeStruct((n * B, 2 * B), BF),
        ),
        in_specs=[smem] * 4
        + [whole(4, 2, 4, SHARD, B)] * 8
        + [
            whole(PS * B, B),
            whole(B, PS * B),
            whole(B, B),
            part((Q + 1) * B, B),
            part(B, (Q + 1) * B),
            part(B, B),
        ],
        out_specs=(
            whole(1, PS, B, B),
            whole(1, B, B),
            part(Q + 1, B, B),
            part(B, B),
            pl.BlockSpec((KIDS * B, 2 * B), lambda i: (jnp.maximum(i - steps, 0), 0)),
        ),
        scratch_shapes=[
            pltpu.VMEM((NA * B, NA * B), BF),
            pltpu.VMEM(((PS + 1) * B, (PS + 1) * B), BF),
            pltpu.VMEM((2 * n * B, B), F32),
            pltpu.VMEM((2 * KIDS * B, B), F32),
        ],
        cost_estimate=pl.CostEstimate(
            flops=720 * 2 * B**3, bytes_accessed=20 * 2**20, transcendentals=0
        ),
        compiler_params=pltpu.CompilerParams(vmem_limit_bytes=48 * 2**20),
        name="late",
    )(me.reshape(1), fidx, spos.reshape(-1), order, *ga, *gb, fu, fut, fw, su, sut, sw)


def along_x(v, k):
    return lax.ppermute(
        v, "col", [(z * 4 + x, z * 4 + (x + k) % 4) for z in range(2) for x in range(4)]
    )


def along_row(v, k):
    return lax.ppermute(v, "row", [(r, (r + k) % 4) for r in range(4)])


def spread(v, move):
    return [v] + [move(v, k) for k in REL[1:]]


def local(
    top_covariance,
    first_panel,
    first_inverse,
    first_index,
    second_panel,
    second_inverse,
    second_positions,
    row_order,
    sensitivity,
):
    me = (lax.axis_index("row") * 8 + lax.axis_index("col")).astype(jnp.int32)
    mine = pack(top_covariance, me)
    other = lax.ppermute(mine, "col", [(c, (c + 4) % 8) for c in range(8)])
    half_a = jnp.stack([mine[0], other[0]])
    half_b = jnp.stack([mine[1], other[1]])
    ga = spread(jnp.stack(spread(half_a, along_x)), along_row)
    gb = spread(jnp.stack(spread(half_b, along_row)), along_x)
    fu, fut, fw, su, sut, sw = early(first_panel, first_inverse, second_panel, second_inverse)
    first_cross, first_diag, second_cross, second_diag, ordered = late(
        me, first_index, second_positions, row_order, ga, gb, fu, fut, fw, su, sut, sw
    )
    received = lax.all_to_all(ordered, ("row", "col"), split_axis=0, concat_axis=0, tiled=True)
    tile_products = jnp.dot(received, sensitivity[0], preferred_element_type=F32).astype(BF)
    return (first_cross, first_diag, second_cross, second_diag, tile_products)


def solution(mesh):
    own = ("grp", "row", "col")
    return jax.shard_map(
        local,
        mesh=mesh,
        in_specs=(
            P(own, None),
            P(own, None, None, None),
            P(own, None, None),
            P(own, None),
            P(own, None, None, None),
            P(own, None, None),
            P(own, None),
            P(own),
            P(own, None, None),
        ),
        out_specs=(
            P(own, None, None, None),
            P(own, None, None),
            P(own, None, None, None),
            P(own, None, None),
            P(own, None),
        ),
        check_vma=False,
    )
```

```python
import functools

import jax
import jax.numpy as jnp
from jax import lax
from jax.experimental import pallas as pl
from jax.experimental.pallas import tpu as pltpu
from jax.sharding import PartitionSpec as P

B = 128
NA = 12
PS = 8
Q = 3
WIN = 8
SHARD = 48
SENT = 4 * SHARD + B
TILES = 32
F32 = jnp.float32
BF = jnp.bfloat16
REL = (0, 1, -1, 2)


def mm(a, b):
    return jnp.dot(a, b, preferred_element_type=F32)


def mm_tn(a, b):
    return lax.dot_general(a, b, (((0,), (0,)), ((), ())), preferred_element_type=F32)


def mm_tt(a, b):
    return lax.dot_general(a, b, (((0,), (1,)), ((), ())), preferred_element_type=F32)


def flip(x):
    return x.astype(F32).T.astype(BF)


def pack_kernel(pos, x_ref, s_ref, o_ref):
    first = (3 * pos[0]) // 8
    for k in range(WIN):
        col = lax.rem(first + k, NA)
        at = (k % 4) * SHARD
        o_ref[k // 4, at:at + SHARD] = x_ref[:, pl.ds(pl.multiple_of(col * B, B), B)]
    for h in range(2):
        o_ref[h, 4 * SHARD:] = s_ref[0, h * B:(h + 1) * B]


def pack(x, sens, me):
    return pl.pallas_call(
        pack_kernel,
        out_shape=jax.ShapeDtypeStruct((2, SENT, B), BF),
        in_specs=[
            pl.BlockSpec(memory_space=pltpu.SMEM),
            pl.BlockSpec(memory_space=pltpu.VMEM),
            pl.BlockSpec(memory_space=pltpu.VMEM),
        ],
        out_specs=pl.BlockSpec(memory_space=pltpu.VMEM),
        name="pack",
    )(me.reshape(1), x, sens)


KIDS = 4
CHUNK = 8


def early_kernel(fp, fi, sp, si, fu, fut, fw, su, sut, sw):
    @pl.when(pl.program_id(0) == 0)
    def _():
        inv = fi[0]
        pan = fp[0].reshape(PS * B, B)
        fu[...] = mm(pan, inv).astype(BF)
        fut[...] = mm_tt(inv, pan).astype(BF)
        fw[...] = mm_tn(inv, inv)

    for c in range(KIDS):
        inv = si[c]
        pan = sp[c].reshape((Q + 1) * B, B)
        su[c] = mm(pan, inv).astype(BF)
        sut[c] = mm_tt(inv, pan).astype(BF)
        sw[c] = mm_tn(inv, inv)


def early(fp, fi, sp, si):
    n = sp.shape[0]
    whole = lambda *s: pl.BlockSpec(s, lambda i: (0,) * len(s))
    part = lambda *s: pl.BlockSpec((KIDS,) + s, lambda i: (i,) + (0,) * len(s))
    return pl.pallas_call(
        early_kernel,
        grid=(n // KIDS,),
        out_shape=(
            jax.ShapeDtypeStruct((PS * B, B), BF),
            jax.ShapeDtypeStruct((B, PS * B), BF),
            jax.ShapeDtypeStruct((B, B), F32),
            jax.ShapeDtypeStruct((n, (Q + 1) * B, B), BF),
            jax.ShapeDtypeStruct((n, B, (Q + 1) * B), BF),
            jax.ShapeDtypeStruct((n, B, B), F32),
        ),
        in_specs=[
            whole(1, PS, B, B),
            whole(1, B, B),
            part(Q + 1, B, B),
            part(B, B),
        ],
        out_specs=(
            whole(PS * B, B),
            whole(B, PS * B),
            whole(B, B),
            part((Q + 1) * B, B),
            part(B, (Q + 1) * B),
            part(B, B),
        ),
        cost_estimate=pl.CostEstimate(
            flops=300 * 2 * B**3, bytes_accessed=20 * 2**20, transcendentals=0
        ),
        compiler_params=pltpu.CompilerParams(vmem_limit_bytes=12 * 2**20),
        name="early",
    )(fp, fi, sp, si)


def late_kernel(
    steps, pos, fidx, spos, order,
    a0, a1, a2, a3, b0, b1, b2, b3, fu, fut, fw, su, sut, sw,
    fc_o, fd_o, sc_o, sd_o, rows_o,
    full, tmat, cov, got, sens, landed, sems,
):
    step = pl.program_id(0)

    @pl.when(step == 0)
    def _():
        me = pos[0]
        row, zh, x = me // 8, (me // 4) % 2, me % 4
        copies = [
            pltpu.make_async_copy(ref, landed.at[n], sems.at[n])
            for n, ref in enumerate((a0, a1, a2, a3, b0, b1, b2, b3))
        ]
        for copy in copies:
            copy.start()
        for half in range(2):
            for t in range(4):
                group = half * 4 + t
                copies[group].wait()
                for u in range(4):
                    dr, dx = (REL[t], REL[u]) if half == 0 else (REL[u], REL[t])
                    r = lax.rem(row - dr + 4, 4)
                    xx = lax.rem(x - dx + 4, 4)
                    for z in range(2):
                        src = r * 8 + lax.rem(zh + z, 2) * 4 + xx
                        first = (3 * src) // 8
                        at = pl.multiple_of(src * SHARD, 16)
                        for k in range(4):
                            col = lax.rem(first + half * 4 + k, NA)
                            full[pl.ds(at, SHARD), pl.ds(pl.multiple_of(col * B, B), B)] = (
                                landed[group, u, z, k * SHARD:(k + 1) * SHARD]
                            )
                        sens[src, half * B:(half + 1) * B] = landed[group, u, z, 4 * SHARD:]

        def block(p, q):
            return full[
                pl.ds(pl.multiple_of(p * B, B), B), pl.ds(pl.multiple_of(q * B, B), B)
            ]

        for p in range(PS):
            ap = fidx[0, p]
            tmat[(1 + p) * B:(2 + p) * B, (1 + p) * B:(2 + p) * B] = block(ap, ap)
            for q in range(p + 1, PS):
                aq = fidx[0, q]
                near = aq - ap <= 6
                i, j = jnp.where(near, p, q), jnp.where(near, q, p)
                held = block(jnp.where(near, ap, aq), jnp.where(near, aq, ap))
                ri = pl.ds(pl.multiple_of((1 + i) * B, B), B)
                rj = pl.ds(pl.multiple_of((1 + j) * B, B), B)
                tmat[ri, rj] = held
                tmat[rj, ri] = flip(held)
        cross = (-mm(tmat[B:, B:], fu[...])).astype(BF)
        fc_o[...] = cross.reshape(1, PS, B, B)
        tmat[B:, :B] = cross
        for p in range(PS):
            tmat[:B, (1 + p) * B:(2 + p) * B] = flip(cross[p * B:(p + 1) * B])
        diag = (fw[...] - mm(fut[...], cross)).astype(BF)
        fd_o[0] = diag
        tmat[:B, :B] = diag

    @pl.when(step < steps)
    def _():
        for c in range(KIDS):
            kid = step * KIDS + c
            at = [0] + [(1 + spos[kid * Q + q]) * B for q in range(Q)]
            at = [pl.ds(pl.multiple_of(v, B), B) for v in at]
            u = su[c]
            ws = []
            for r in range(Q + 1):
                line = jnp.concatenate([tmat[at[r], at[q]] for q in range(Q + 1)], axis=1)
                w = (-mm(line, u)).astype(BF)
                sc_o[c, r] = w
                ws.append(w)
            d = (sw[c] - mm(sut[c], jnp.concatenate(ws, axis=0))).astype(BF)
            sd_o[c] = d
            base = pl.multiple_of(kid * 2 * B, 2 * B)
            cov[pl.ds(base, B, stride=2), :] = d.astype(F32)
            cov[pl.ds(base + 1, B, stride=2), :] = ws[0].astype(F32)

    @pl.when(step == steps)
    def _():
        rows = CHUNK * B

        def chunk(k, carry):
            def move(g, inner):
                for j in range(16):
                    src = order[k * rows + g * 16 + j]
                    got[pl.ds(pl.multiple_of(g * 32, 32) + 2 * j, 2), :] = cov[
                        pl.ds(pl.multiple_of(src * 2, 2), 2), :
                    ]
                return inner

            lax.fori_loop(0, rows // 16, move, 0)
            for t in range(CHUNK):
                line = jnp.concatenate(
                    [
                        got[pl.ds(t * 2 * B, B, stride=2), :],
                        got[pl.ds(t * 2 * B + 1, B, stride=2), :],
                    ],
                    axis=1,
                ).astype(BF)
                at = pl.multiple_of((k * CHUNK + t) * B, B)
                rows_o[pl.ds(at, B)] = mm(line, sens[k * CHUNK + t]).astype(BF)
            return carry

        lax.fori_loop(0, TILES // CHUNK, chunk, 0)


def late(me, fidx, spos, order, ga, gb, fu, fut, fw, su, sut, sw):
    n = su.shape[0]
    steps = n // KIDS
    whole = lambda *s: pl.BlockSpec(s, lambda i: (0,) * len(s))
    part = lambda *s: pl.BlockSpec(
        (KIDS,) + s, lambda i: (jnp.minimum(i, steps - 1),) + (0,) * len(s)
    )
    smem = pl.BlockSpec(memory_space=pltpu.SMEM)
    return pl.pallas_call(
        functools.partial(late_kernel, steps),
        grid=(steps + 1,),
        out_shape=(
            jax.ShapeDtypeStruct((1, PS, B, B), BF),
            jax.ShapeDtypeStruct((1, B, B), BF),
            jax.ShapeDtypeStruct((n, Q + 1, B, B), BF),
            jax.ShapeDtypeStruct((n, B, B), BF),
            jax.ShapeDtypeStruct((n * B, B), BF),
        ),
        in_specs=[smem] * 4
        + [pl.BlockSpec(memory_space=pl.ANY)] * 8
        + [
            whole(PS * B, B),
            whole(B, PS * B),
            whole(B, B),
            part((Q + 1) * B, B),
            part(B, (Q + 1) * B),
            part(B, B),
        ],
        out_specs=(
            whole(1, PS, B, B),
            whole(1, B, B),
            part(Q + 1, B, B),
            part(B, B),
            whole(n * B, B),
        ),
        scratch_shapes=[
            pltpu.VMEM((NA * B, NA * B), BF),
            pltpu.VMEM(((PS + 1) * B, (PS + 1) * B), BF),
            pltpu.VMEM((2 * n * B, B), F32),
            pltpu.VMEM((2 * CHUNK * B, B), F32),
            pltpu.VMEM((TILES, 2 * B, B), BF),
            pltpu.VMEM((8, 4, 2, SENT, B), BF),
            pltpu.SemaphoreType.DMA((8,)),
        ],
        cost_estimate=pl.CostEstimate(
            flops=720 * 2 * B**3, bytes_accessed=20 * 2**20, transcendentals=0
        ),
        compiler_params=pltpu.CompilerParams(vmem_limit_bytes=30 * 2**20),
        name="late",
    )(me.reshape(1), fidx, spos.reshape(-1), order, *ga, *gb, fu, fut, fw, su, sut, sw)


def along_x(v, k):
    return lax.ppermute(
        v, "col", [(z * 4 + x, z * 4 + (x + k) % 4) for z in range(2) for x in range(4)]
    )


def along_row(v, k):
    return lax.ppermute(v, "row", [(r, (r + k) % 4) for r in range(4)])


def spread(v, move):
    return [v] + [move(v, k) for k in REL[1:]]


def local(
    top_covariance,
    first_panel,
    first_inverse,
    first_index,
    second_panel,
    second_inverse,
    second_positions,
    row_order,
    sensitivity,
):
    me = (lax.axis_index("row") * 8 + lax.axis_index("col")).astype(jnp.int32)
    fixed = lax.optimization_barrier
    mine = pack(top_covariance, sensitivity, me)
    other = lax.ppermute(mine, "col", [(c, (c + 4) % 8) for c in range(8)])
    half_a, half_b = fixed((jnp.stack([mine[0], other[0]]), jnp.stack([mine[1], other[1]])))
    near_a, near_b = fixed((spread(half_a, along_x), spread(half_b, along_row)))
    near_a, near_b = fixed((jnp.stack(near_a), jnp.stack(near_b)))
    ga, gb = spread(near_a, along_row), spread(near_b, along_x)
    fu, fut, fw, su, sut, sw = early(first_panel, first_inverse, second_panel, second_inverse)
    first_cross, first_diag, second_cross, second_diag, products = late(
        me, first_index, second_positions, row_order, ga, gb, fu, fut, fw, su, sut, sw
    )
    tile_products = lax.all_to_all(
        products, ("row", "col"), split_axis=0, concat_axis=0, tiled=True
    )
    return (first_cross, first_diag, second_cross, second_diag, tile_products)


def solution(mesh):
    own = ("grp", "row", "col")
    return jax.shard_map(
        local,
        mesh=mesh,
        in_specs=(
            P(own, None),
            P(own, None, None, None),
            P(own, None, None),
            P(own, None),
            P(own, None, None, None),
            P(own, None, None),
            P(own, None),
            P(own),
            P(own, None, None),
        ),
        out_specs=(
            P(own, None, None, None),
            P(own, None, None),
            P(own, None, None, None),
            P(own, None, None),
            P(own, None),
        ),
        check_vma=False,
    )
```

```python
import functools

import jax
import jax.numpy as jnp
from jax import lax
from jax.experimental import pallas as pl
from jax.experimental.pallas import tpu as pltpu
from jax.sharding import PartitionSpec as P

B = 128
NA = 12
PS = 8
Q = 3
WIN = 8
SHARD = 48
SENT = 4 * SHARD + B
TILES = 32
F32 = jnp.float32
BF = jnp.bfloat16
REL = (0, 1, -1, 2)


def mm(a, b):
    return jnp.dot(a, b, preferred_element_type=F32)


def mm_tn(a, b):
    return lax.dot_general(a, b, (((0,), (0,)), ((), ())), preferred_element_type=F32)


def mm_tt(a, b):
    return lax.dot_general(a, b, (((0,), (1,)), ((), ())), preferred_element_type=F32)


def flip(x):
    return x.astype(F32).T.astype(BF)


def pack_kernel(pos, x_ref, s_ref, o_ref):
    first = (3 * pos[0]) // 8
    for k in range(WIN):
        col = lax.rem(first + k, NA)
        at = (k % 4) * SHARD
        o_ref[k // 4, at:at + SHARD] = x_ref[:, pl.ds(pl.multiple_of(col * B, B), B)]
    for h in range(2):
        o_ref[h, 4 * SHARD:] = s_ref[0, h * B:(h + 1) * B]


def pack(x, sens, me):
    return pl.pallas_call(
        pack_kernel,
        out_shape=jax.ShapeDtypeStruct((2, SENT, B), BF),
        in_specs=[
            pl.BlockSpec(memory_space=pltpu.SMEM),
            pl.BlockSpec(memory_space=pltpu.VMEM),
            pl.BlockSpec(memory_space=pltpu.VMEM),
        ],
        out_specs=pl.BlockSpec(memory_space=pltpu.VMEM),
        name="pack",
    )(me.reshape(1), x, sens)


KIDS = 8


def early_kernel(fp, fi, sp, si, fu, fut, fw, su, sut, sw):
    @pl.when(pl.program_id(0) == 0)
    def _():
        inv = fi[0]
        pan = fp[0].reshape(PS * B, B)
        fu[...] = mm(pan, inv).astype(BF)
        fut[...] = mm_tt(inv, pan).astype(BF)
        fw[...] = mm_tn(inv, inv)

    for c in range(KIDS):
        inv = si[c]
        pan = sp[c].reshape((Q + 1) * B, B)
        su[c] = mm(pan, inv).astype(BF)
        sut[c] = mm_tt(inv, pan).astype(BF)
        sw[c] = mm_tn(inv, inv)


def early(fp, fi, sp, si):
    n = sp.shape[0]
    whole = lambda *s: pl.BlockSpec(s, lambda i: (0,) * len(s))
    part = lambda *s: pl.BlockSpec((KIDS,) + s, lambda i: (i,) + (0,) * len(s))
    return pl.pallas_call(
        early_kernel,
        grid=(n // KIDS,),
        out_shape=(
            jax.ShapeDtypeStruct((PS * B, B), BF),
            jax.ShapeDtypeStruct((B, PS * B), BF),
            jax.ShapeDtypeStruct((B, B), F32),
            jax.ShapeDtypeStruct((n, (Q + 1) * B, B), BF),
            jax.ShapeDtypeStruct((n, B, (Q + 1) * B), BF),
            jax.ShapeDtypeStruct((n, B, B), F32),
        ),
        in_specs=[
            whole(1, PS, B, B),
            whole(1, B, B),
            part(Q + 1, B, B),
            part(B, B),
        ],
        out_specs=(
            whole(PS * B, B),
            whole(B, PS * B),
            whole(B, B),
            part((Q + 1) * B, B),
            part(B, (Q + 1) * B),
            part(B, B),
        ),
        cost_estimate=pl.CostEstimate(
            flops=300 * 2 * B**3, bytes_accessed=20 * 2**20, transcendentals=0
        ),
        compiler_params=pltpu.CompilerParams(vmem_limit_bytes=12 * 2**20),
        name="early",
    )(fp, fi, sp, si)


def late_kernel(
    steps, pos, fidx, spos, order,
    a0, a1, a2, a3, b0, b1, b2, b3, fu, fut, fw, su, sut, sw,
    fc_o, fd_o, sc_o, sd_o, rows_o,
    full, tmat, cov, even, odd, sens, landed, sems,
):
    step = pl.program_id(0)

    @pl.when(step == 0)
    def _():
        me = pos[0]
        row, zh, x = me // 8, (me // 4) % 2, me % 4
        copies = [
            pltpu.make_async_copy(ref, landed.at[n], sems.at[n])
            for n, ref in enumerate((a0, a1, a2, a3, b0, b1, b2, b3))
        ]
        for copy in copies:
            copy.start()
        for half in range(2):
            for t in range(4):
                group = half * 4 + t
                copies[group].wait()
                for u in range(4):
                    dr, dx = (REL[t], REL[u]) if half == 0 else (REL[u], REL[t])
                    r = lax.rem(row - dr + 4, 4)
                    xx = lax.rem(x - dx + 4, 4)
                    for z in range(2):
                        src = r * 8 + lax.rem(zh + z, 2) * 4 + xx
                        first = (3 * src) // 8
                        at = pl.multiple_of(src * SHARD, 16)
                        for k in range(4):
                            col = lax.rem(first + half * 4 + k, NA)
                            full[pl.ds(at, SHARD), pl.ds(pl.multiple_of(col * B, B), B)] = (
                                landed[group, u, z, k * SHARD:(k + 1) * SHARD]
                            )
                        sens[src, half * B:(half + 1) * B] = landed[group, u, z, 4 * SHARD:]

        def block(p, q):
            return full[
                pl.ds(pl.multiple_of(p * B, B), B), pl.ds(pl.multiple_of(q * B, B), B)
            ]

        for p in range(PS):
            ap = fidx[0, p]
            tmat[(1 + p) * B:(2 + p) * B, (1 + p) * B:(2 + p) * B] = block(ap, ap)
            for q in range(p + 1, PS):
                aq = fidx[0, q]
                near = aq - ap <= 6
                i, j = jnp.where(near, p, q), jnp.where(near, q, p)
                held = block(jnp.where(near, ap, aq), jnp.where(near, aq, ap))
                ri = pl.ds(pl.multiple_of((1 + i) * B, B), B)
                rj = pl.ds(pl.multiple_of((1 + j) * B, B), B)
                tmat[ri, rj] = held
                tmat[rj, ri] = flip(held)
        cross = (-mm(tmat[B:, B:], fu[...])).astype(BF)
        fc_o[...] = cross.reshape(1, PS, B, B)
        tmat[B:, :B] = cross
        for p in range(PS):
            tmat[:B, (1 + p) * B:(2 + p) * B] = flip(cross[p * B:(p + 1) * B])
        diag = (fw[...] - mm(fut[...], cross)).astype(BF)
        fd_o[0] = diag
        tmat[:B, :B] = diag

    @pl.when(step < steps)
    def _():
        for c in range(KIDS):
            kid = step * KIDS + c
            at = [0] + [(1 + spos[kid * Q + q]) * B for q in range(Q)]
            at = [pl.ds(pl.multiple_of(v, B), B) for v in at]
            for r in range(Q + 1):
                line = jnp.concatenate([tmat[at[r], at[q]] for q in range(Q + 1)], axis=1)
                sc_o[c, r] = (-mm(line, su[c])).astype(BF)
        for c in range(KIDS):
            w = sc_o[c].reshape((Q + 1) * B, B)
            d = (sw[c] - mm(sut[c], w)).astype(BF)
            sd_o[c] = d
            base = pl.multiple_of((step * KIDS + c) * 2 * B, 2 * B)
            cov[pl.ds(base, B, stride=2), :] = d.astype(F32)
            cov[pl.ds(base + 1, B, stride=2), :] = w[:B].astype(F32)

    @pl.when(step == steps)
    def _():
        def move(t, got):
            for m in range(B):
                src = order[t * B + m]
                got[2 * m:2 * m + 2, :] = cov[pl.ds(pl.multiple_of(src * 2, 2), 2), :]

        def product(t, got):
            line = jnp.concatenate(
                [got[pl.ds(0, B, stride=2), :], got[pl.ds(1, B, stride=2), :]], axis=1
            ).astype(BF)
            rows_o[pl.ds(pl.multiple_of(t * B, B), B)] = mm(line, sens[t]).astype(BF)

        move(0, even)

        def pair(i, carry):
            move(2 * i + 1, odd)
            product(2 * i, even)
            move(jnp.minimum(2 * i + 2, TILES - 1), even)
            product(2 * i + 1, odd)
            return carry

        lax.fori_loop(0, TILES // 2, pair, 0)


def late(me, fidx, spos, order, ga, gb, fu, fut, fw, su, sut, sw):
    n = su.shape[0]
    steps = n // KIDS
    whole = lambda *s: pl.BlockSpec(s, lambda i: (0,) * len(s))
    part = lambda *s: pl.BlockSpec(
        (KIDS,) + s, lambda i: (jnp.minimum(i, steps - 1),) + (0,) * len(s)
    )
    smem = pl.BlockSpec(memory_space=pltpu.SMEM)
    return pl.pallas_call(
        functools.partial(late_kernel, steps),
        grid=(steps + 1,),
        out_shape=(
            jax.ShapeDtypeStruct((1, PS, B, B), BF),
            jax.ShapeDtypeStruct((1, B, B), BF),
            jax.ShapeDtypeStruct((n, Q + 1, B, B), BF),
            jax.ShapeDtypeStruct((n, B, B), BF),
            jax.ShapeDtypeStruct((n * B, B), BF),
        ),
        in_specs=[smem] * 4
        + [pl.BlockSpec(memory_space=pl.ANY)] * 8
        + [
            whole(PS * B, B),
            whole(B, PS * B),
            whole(B, B),
            part((Q + 1) * B, B),
            part(B, (Q + 1) * B),
            part(B, B),
        ],
        out_specs=(
            whole(1, PS, B, B),
            whole(1, B, B),
            part(Q + 1, B, B),
            part(B, B),
            whole(n * B, B),
        ),
        scratch_shapes=[
            pltpu.VMEM((NA * B, NA * B), BF),
            pltpu.VMEM(((PS + 1) * B, (PS + 1) * B), BF),
            pltpu.VMEM((2 * n * B, B), F32),
            pltpu.VMEM((2 * B, B), F32),
            pltpu.VMEM((2 * B, B), F32),
            pltpu.VMEM((TILES, 2 * B, B), BF),
            pltpu.VMEM((8, 4, 2, SENT, B), BF),
            pltpu.SemaphoreType.DMA((8,)),
        ],
        cost_estimate=pl.CostEstimate(
            flops=720 * 2 * B**3, bytes_accessed=20 * 2**20, transcendentals=0
        ),
        compiler_params=pltpu.CompilerParams(vmem_limit_bytes=30 * 2**20),
        name="late",
    )(me.reshape(1), fidx, spos.reshape(-1), order, *ga, *gb, fu, fut, fw, su, sut, sw)


def along_x(v, k):
    return lax.ppermute(
        v, "col", [(z * 4 + x, z * 4 + (x + k) % 4) for z in range(2) for x in range(4)]
    )


def along_row(v, k):
    return lax.ppermute(v, "row", [(r, (r + k) % 4) for r in range(4)])


def spread(v, move):
    return [v] + [move(v, k) for k in REL[1:]]


def local(
    top_covariance,
    first_panel,
    first_inverse,
    first_index,
    second_panel,
    second_inverse,
    second_positions,
    row_order,
    sensitivity,
):
    me = (lax.axis_index("row") * 8 + lax.axis_index("col")).astype(jnp.int32)
    fixed = lax.optimization_barrier
    mine = pack(top_covariance, sensitivity, me)
    other = lax.ppermute(mine, "col", [(c, (c + 4) % 8) for c in range(8)])
    half_a, half_b = fixed((jnp.stack([mine[0], other[0]]), jnp.stack([mine[1], other[1]])))
    near_a, near_b = fixed((spread(half_a, along_x), spread(half_b, along_row)))
    near_a, near_b = fixed((jnp.stack(near_a), jnp.stack(near_b)))
    ga, gb = spread(near_a, along_row), spread(near_b, along_x)
    fu, fut, fw, su, sut, sw = early(first_panel, first_inverse, second_panel, second_inverse)
    first_cross, first_diag, second_cross, second_diag, products = late(
        me, first_index, second_positions, row_order, ga, gb, fu, fut, fw, su, sut, sw
    )
    tile_products = lax.all_to_all(
        products, ("row", "col"), split_axis=0, concat_axis=0, tiled=True
    )
    return (first_cross, first_diag, second_cross, second_diag, tile_products)


def solution(mesh):
    own = ("grp", "row", "col")
    return jax.shard_map(
        local,
        mesh=mesh,
        in_specs=(
            P(own, None),
            P(own, None, None, None),
            P(own, None, None),
            P(own, None),
            P(own, None, None, None),
            P(own, None, None),
            P(own, None),
            P(own),
            P(own, None, None),
        ),
        out_specs=(
            P(own, None, None, None),
            P(own, None, None),
            P(own, None, None, None),
            P(own, None, None),
            P(own, None),
        ),
        check_vma=False,
    )
```

```python
import jax
import jax.numpy as jnp
from jax import lax
from jax.experimental import pallas as pl
from jax.experimental.pallas import tpu as pltpu
from jax.sharding import PartitionSpec as P

B = 128
NA = 12
PS = 8
Q = 3
WIN = 8
SHARD = 48
PART = 4 * SHARD
SENT = PART + B
TILES = 32
F32 = jnp.float32
BF = jnp.bfloat16
REL = (0, 1, -1, 2)


def mm(a, b):
    return jnp.dot(a, b, preferred_element_type=F32)


def mm_tn(a, b):
    return lax.dot_general(a, b, (((0,), (0,)), ((), ())), preferred_element_type=F32)


def mm_tt(a, b):
    return lax.dot_general(a, b, (((0,), (1,)), ((), ())), preferred_element_type=F32)


def flip(x):
    return x.astype(F32).T.astype(BF)


def pack_kernel(pos, x_ref, s_ref, o_ref):
    first = (3 * pos[0]) // 8
    for k in range(WIN):
        col = lax.rem(first + k, NA)
        at = (k % 4) * SHARD
        o_ref[k // 4, at:at + SHARD] = x_ref[:, pl.ds(pl.multiple_of(col * B, B), B)]
    for h in range(2):
        o_ref[h, 4 * SHARD:] = s_ref[0, h * B:(h + 1) * B]


def pack(x, sens, me):
    return pl.pallas_call(
        pack_kernel,
        out_shape=jax.ShapeDtypeStruct((2, SENT, B), BF),
        in_specs=[
            pl.BlockSpec(memory_space=pltpu.SMEM),
            pl.BlockSpec(memory_space=pltpu.VMEM),
            pl.BlockSpec(memory_space=pltpu.VMEM),
        ],
        out_specs=pl.BlockSpec(memory_space=pltpu.VMEM),
        name="pack",
    )(me.reshape(1), x, sens)


def sort_near_kernel(*refs):
    parts, outs, sems = refs[:8], refs[8:12], refs[12]
    copies = []
    for n, ref in enumerate(parts):
        half, t = n // 4, n % 4
        copies += [
            pltpu.make_async_copy(ref.at[:, pl.ds(0, PART)], outs[half].at[t], sems.at[n]),
            pltpu.make_async_copy(ref.at[:, pl.ds(PART, B)], outs[2 + half].at[t], sems.at[8 + n]),
        ]
    for copy in copies:
        copy.start()
    for copy in copies:
        copy.wait()


def sort_near(near_a, near_b):
    any_ = pl.BlockSpec(memory_space=pl.ANY)
    return pl.pallas_call(
        sort_near_kernel,
        out_shape=[jax.ShapeDtypeStruct((4, 2, n, B), BF) for n in (PART, PART, B, B)],
        in_specs=[any_] * 8,
        out_specs=[any_] * 4,
        scratch_shapes=[pltpu.SemaphoreType.DMA((16,))],
        compiler_params=pltpu.CompilerParams(vmem_limit_bytes=2**20),
        name="sort_near",
    )(*near_a, *near_b)


KIDS = 8


def early_kernel(fp, fi, sp, si, fu, fut, fw, su, sut, sw):
    @pl.when(pl.program_id(0) == 0)
    def _():
        inv = fi[0]
        pan = fp[0].reshape(PS * B, B)
        fu[...] = mm(pan, inv).astype(BF)
        fut[...] = mm_tt(inv, pan).astype(BF)
        fw[...] = mm_tn(inv, inv)

    for c in range(KIDS):
        inv = si[c]
        pan = sp[c].reshape((Q + 1) * B, B)
        su[c] = mm(pan, inv).astype(BF)
        sut[c] = mm_tt(inv, pan).astype(BF)
        sw[c] = mm_tn(inv, inv)


def early(fp, fi, sp, si):
    n = sp.shape[0]
    whole = lambda *s: pl.BlockSpec(s, lambda i: (0,) * len(s))
    part = lambda *s: pl.BlockSpec((KIDS,) + s, lambda i: (i,) + (0,) * len(s))
    return pl.pallas_call(
        early_kernel,
        grid=(n // KIDS,),
        out_shape=(
            jax.ShapeDtypeStruct((PS * B, B), BF),
            jax.ShapeDtypeStruct((B, PS * B), BF),
            jax.ShapeDtypeStruct((B, B), F32),
            jax.ShapeDtypeStruct((n, (Q + 1) * B, B), BF),
            jax.ShapeDtypeStruct((n, B, (Q + 1) * B), BF),
            jax.ShapeDtypeStruct((n, B, B), F32),
        ),
        in_specs=[
            whole(1, PS, B, B),
            whole(1, B, B),
            part(Q + 1, B, B),
            part(B, B),
        ],
        out_specs=(
            whole(PS * B, B),
            whole(B, PS * B),
            whole(B, B),
            part((Q + 1) * B, B),
            part(B, (Q + 1) * B),
            part(B, B),
        ),
        cost_estimate=pl.CostEstimate(
            flops=300 * 2 * B**3, bytes_accessed=20 * 2**20, transcendentals=0
        ),
        compiler_params=pltpu.CompilerParams(vmem_limit_bytes=12 * 2**20),
        name="early",
    )(fp, fi, sp, si)


def late_kernel(
    pos, fidx, spos,
    a0, a1, a2, a3, b0, b1, b2, b3, fu, fut, fw, su, sut, sw,
    fc_o, fd_o, sc_o, sd_o, cov_o,
    full, tmat, landed, sems,
):
    step = pl.program_id(0)

    @pl.when(step == 0)
    def _():
        me = pos[0]
        row, zh, x = me // 8, (me // 4) % 2, me % 4
        copies = [
            pltpu.make_async_copy(ref, landed.at[n], sems.at[n])
            for n, ref in enumerate((a0, a1, a2, a3, b0, b1, b2, b3))
        ]
        for copy in copies:
            copy.start()
        for half in range(2):
            for t in range(4):
                group = half * 4 + t
                copies[group].wait()
                for u in range(4):
                    dr, dx = (REL[t], REL[u]) if half == 0 else (REL[u], REL[t])
                    r = lax.rem(row - dr + 4, 4)
                    xx = lax.rem(x - dx + 4, 4)
                    for z in range(2):
                        src = r * 8 + lax.rem(zh + z, 2) * 4 + xx
                        first = (3 * src) // 8
                        at = pl.multiple_of(src * SHARD, 16)
                        for k in range(4):
                            col = lax.rem(first + half * 4 + k, NA)
                            full[pl.ds(at, SHARD), pl.ds(pl.multiple_of(col * B, B), B)] = (
                                landed[group, u, z, k * SHARD:(k + 1) * SHARD]
                            )

        def block(p, q):
            return full[
                pl.ds(pl.multiple_of(p * B, B), B), pl.ds(pl.multiple_of(q * B, B), B)
            ]

        for p in range(PS):
            ap = fidx[0, p]
            tmat[(1 + p) * B:(2 + p) * B, (1 + p) * B:(2 + p) * B] = block(ap, ap)
            for q in range(p + 1, PS):
                aq = fidx[0, q]
                near = aq - ap <= 6
                i, j = jnp.where(near, p, q), jnp.where(near, q, p)
                held = block(jnp.where(near, ap, aq), jnp.where(near, aq, ap))
                ri = pl.ds(pl.multiple_of((1 + i) * B, B), B)
                rj = pl.ds(pl.multiple_of((1 + j) * B, B), B)
                tmat[ri, rj] = held
                tmat[rj, ri] = flip(held)
        cross = (-mm(tmat[B:, B:], fu[...])).astype(BF)
        fc_o[...] = cross.reshape(1, PS, B, B)
        tmat[B:, :B] = cross
        for p in range(PS):
            tmat[:B, (1 + p) * B:(2 + p) * B] = flip(cross[p * B:(p + 1) * B])
        diag = (fw[...] - mm(fut[...], cross)).astype(BF)
        fd_o[0] = diag
        tmat[:B, :B] = diag

    for c in range(KIDS):
        kid = step * KIDS + c
        at = [0] + [(1 + spos[kid * Q + q]) * B for q in range(Q)]
        at = [pl.ds(pl.multiple_of(v, B), B) for v in at]
        for r in range(Q + 1):
            line = jnp.concatenate([tmat[at[r], at[q]] for q in range(Q + 1)], axis=1)
            sc_o[c, r] = (-mm(line, su[c])).astype(BF)
    for c in range(KIDS):
        w = sc_o[c].reshape((Q + 1) * B, B)
        d = (sw[c] - mm(sut[c], w)).astype(BF)
        sd_o[c] = d
        cov_o[pl.ds(c * 2 * B, B, stride=2), :] = d.astype(F32)
        cov_o[pl.ds(c * 2 * B + 1, B, stride=2), :] = w[:B].astype(F32)


def final_kernel(
    pos, order, a0, a1, a2, a3, b0, b1, b2, b3, cov_in, rows_o, cov, even, odd, landed, sems
):
    me = pos[0]
    whole = pltpu.make_async_copy(cov_in, cov, sems.at[8])
    whole.start()
    copies = [
        pltpu.make_async_copy(ref, landed.at[n], sems.at[n])
        for n, ref in enumerate((a0, a1, a2, a3, b0, b1, b2, b3))
    ]
    for copy in copies:
        copy.start()
    whole.wait()

    def place(diff):
        diff = lax.rem(diff + 4, 4)
        return jnp.where(diff < 2, diff, 5 - diff)

    def move(t, got):
        for m in range(B):
            src = order[t * B + m]
            got[2 * m:2 * m + 2, :] = cov[pl.ds(pl.multiple_of(src * 2, 2), 2), :]

    def product(t, got):
        line = jnp.concatenate(
            [got[pl.ds(0, B, stride=2), :], got[pl.ds(1, B, stride=2), :]], axis=1
        ).astype(BF)
        by_row = place(me // 8 - t // 8)
        by_x = place(me % 4 - t % 4)
        z = lax.rem((me // 4) % 2 + (t // 4) % 2, 2)
        sens = jnp.concatenate([landed[by_row, by_x, z], landed[4 + by_x, by_row, z]], axis=0)
        rows_o[pl.ds(pl.multiple_of(t * B, B), B)] = mm(line, sens).astype(BF)

    move(0, even)
    for copy in copies:
        copy.wait()

    def pair(i, carry):
        move(2 * i + 1, odd)
        product(2 * i, even)
        move(jnp.minimum(2 * i + 2, TILES - 1), even)
        product(2 * i + 1, odd)
        return carry

    lax.fori_loop(0, TILES // 2, pair, 0)


def final(me, order, ta, tb, cov):
    smem = pl.BlockSpec(memory_space=pltpu.SMEM)
    n = cov.shape[0]
    return pl.pallas_call(
        final_kernel,
        out_shape=jax.ShapeDtypeStruct((n // 2, B), BF),
        in_specs=[smem] * 2 + [pl.BlockSpec(memory_space=pl.ANY)] * 9,
        out_specs=pl.BlockSpec(memory_space=pltpu.VMEM),
        scratch_shapes=[
            pltpu.VMEM((n, B), F32),
            pltpu.VMEM((2 * B, B), F32),
            pltpu.VMEM((2 * B, B), F32),
            pltpu.VMEM((8, 4, 2, B, B), BF),
            pltpu.SemaphoreType.DMA((9,)),
        ],
        cost_estimate=pl.CostEstimate(
            flops=64 * 2 * B**3, bytes_accessed=12 * 2**20, transcendentals=0
        ),
        compiler_params=pltpu.CompilerParams(vmem_limit_bytes=12 * 2**20),
        name="final",
    )(me.reshape(1), order, *ta, *tb, cov)


def late(me, fidx, spos, ga, gb, fu, fut, fw, su, sut, sw):
    n = su.shape[0]
    steps = n // KIDS
    whole = lambda *s: pl.BlockSpec(s, lambda i: (0,) * len(s))
    part = lambda *s: pl.BlockSpec(
        (KIDS,) + s, lambda i: (i,) + (0,) * len(s)
    )
    smem = pl.BlockSpec(memory_space=pltpu.SMEM)
    return pl.pallas_call(
        late_kernel,
        grid=(steps,),
        out_shape=(
            jax.ShapeDtypeStruct((1, PS, B, B), BF),
            jax.ShapeDtypeStruct((1, B, B), BF),
            jax.ShapeDtypeStruct((n, Q + 1, B, B), BF),
            jax.ShapeDtypeStruct((n, B, B), BF),
            jax.ShapeDtypeStruct((2 * n * B, B), F32),
        ),
        in_specs=[smem] * 3
        + [pl.BlockSpec(memory_space=pl.ANY)] * 8
        + [
            whole(PS * B, B),
            whole(B, PS * B),
            whole(B, B),
            part((Q + 1) * B, B),
            part(B, (Q + 1) * B),
            part(B, B),
        ],
        out_specs=(
            whole(1, PS, B, B),
            whole(1, B, B),
            part(Q + 1, B, B),
            part(B, B),
            pl.BlockSpec((2 * KIDS * B, B), lambda i: (i, 0)),
        ),
        scratch_shapes=[
            pltpu.VMEM((NA * B, NA * B), BF),
            pltpu.VMEM(((PS + 1) * B, (PS + 1) * B), BF),
            pltpu.VMEM((8, 4, 2, PART, B), BF),
            pltpu.SemaphoreType.DMA((8,)),
        ],
        cost_estimate=pl.CostEstimate(
            flops=720 * 2 * B**3, bytes_accessed=32 * 2**20, transcendentals=0
        ),
        compiler_params=pltpu.CompilerParams(vmem_limit_bytes=26 * 2**20),
        name="late",
    )(me.reshape(1), fidx, spos.reshape(-1), *ga, *gb, fu, fut, fw, su, sut, sw)


def along_x(v, k):
    return lax.ppermute(
        v, "col", [(z * 4 + x, z * 4 + (x + k) % 4) for z in range(2) for x in range(4)]
    )


def along_row(v, k):
    return lax.ppermute(v, "row", [(r, (r + k) % 4) for r in range(4)])


def spread(v, move):
    return [v] + [move(v, k) for k in REL[1:]]


def local(
    top_covariance,
    first_panel,
    first_inverse,
    first_index,
    second_panel,
    second_inverse,
    second_positions,
    row_order,
    sensitivity,
):
    me = (lax.axis_index("row") * 8 + lax.axis_index("col")).astype(jnp.int32)
    fixed = lax.optimization_barrier
    mine = pack(top_covariance, sensitivity, me)
    other = lax.ppermute(mine, "col", [(c, (c + 4) % 8) for c in range(8)])
    half_a, half_b = fixed((jnp.stack([mine[0], other[0]]), jnp.stack([mine[1], other[1]])))
    near_a, near_b = fixed((spread(half_a, along_x), spread(half_b, along_row)))
    near_a, near_b, sens_a, sens_b = sort_near(near_a, near_b)
    ga, gb = spread(near_a, along_row), spread(near_b, along_x)
    sens_a, sens_b, ga = fixed((sens_a, sens_b, ga))
    ta, tb = spread(sens_a, along_row), spread(sens_b, along_x)
    fu, fut, fw, su, sut, sw = early(first_panel, first_inverse, second_panel, second_inverse)
    first_cross, first_diag, second_cross, second_diag, cov = late(
        me, first_index, second_positions, ga, gb, fu, fut, fw, su, sut, sw
    )
    products = final(me, row_order, ta, tb, cov)
    tile_products = lax.all_to_all(
        products, ("row", "col"), split_axis=0, concat_axis=0, tiled=True
    )
    return (first_cross, first_diag, second_cross, second_diag, tile_products)


def solution(mesh):
    own = ("grp", "row", "col")
    return jax.shard_map(
        local,
        mesh=mesh,
        in_specs=(
            P(own, None),
            P(own, None, None, None),
            P(own, None, None),
            P(own, None),
            P(own, None, None, None),
            P(own, None, None),
            P(own, None),
            P(own),
            P(own, None, None),
        ),
        out_specs=(
            P(own, None, None, None),
            P(own, None, None),
            P(own, None, None, None),
            P(own, None, None),
            P(own, None),
        ),
        check_vma=False,
    )
```

```python
import jax
import jax.numpy as jnp
from jax import lax
from jax.experimental import pallas as pl
from jax.experimental.pallas import tpu as pltpu
from jax.sharding import PartitionSpec as P

B = 128
NA = 12
PS = 8
Q = 3
WIN = 8
SHARD = 48
PART = 4 * SHARD
SENT = PART + B
TILES = 32
F32 = jnp.float32
BF = jnp.bfloat16
REL = (0, 1, -1, 2)


def mm(a, b):
    return jnp.dot(a, b, preferred_element_type=F32)


def mm_tn(a, b):
    return lax.dot_general(a, b, (((0,), (0,)), ((), ())), preferred_element_type=F32)


def mm_tt(a, b):
    return lax.dot_general(a, b, (((0,), (1,)), ((), ())), preferred_element_type=F32)


def flip(x):
    return x.astype(F32).T.astype(BF)


def pack_kernel(pos, x_ref, s_ref, o_ref):
    first = (3 * pos[0]) // 8
    for k in range(WIN):
        col = lax.rem(first + k, NA)
        at = (k % 4) * SHARD
        o_ref[k // 4, at:at + SHARD] = x_ref[:, pl.ds(pl.multiple_of(col * B, B), B)]
    for h in range(2):
        o_ref[h, 4 * SHARD:] = s_ref[0, h * B:(h + 1) * B]


def pack(x, sens, me):
    return pl.pallas_call(
        pack_kernel,
        out_shape=jax.ShapeDtypeStruct((2, SENT, B), BF),
        in_specs=[
            pl.BlockSpec(memory_space=pltpu.SMEM),
            pl.BlockSpec(memory_space=pltpu.VMEM),
            pl.BlockSpec(memory_space=pltpu.VMEM),
        ],
        out_specs=pl.BlockSpec(memory_space=pltpu.VMEM),
        name="pack",
    )(me.reshape(1), x, sens)


def sort_near_kernel(*refs):
    parts, outs, sems = refs[:8], refs[8:12], refs[12]
    copies = []
    for n, ref in enumerate(parts):
        half, t = n // 4, n % 4
        copies += [
            pltpu.make_async_copy(ref.at[:, pl.ds(0, PART)], outs[half].at[t], sems.at[n]),
            pltpu.make_async_copy(ref.at[:, pl.ds(PART, B)], outs[2 + half].at[t], sems.at[8 + n]),
        ]
    for copy in copies:
        copy.start()
    for copy in copies:
        copy.wait()


def sort_near(near_a, near_b):
    any_ = pl.BlockSpec(memory_space=pl.ANY)
    return pl.pallas_call(
        sort_near_kernel,
        out_shape=[jax.ShapeDtypeStruct((4, 2, n, B), BF) for n in (PART, PART, B, B)],
        in_specs=[any_] * 8,
        out_specs=[any_] * 4,
        scratch_shapes=[pltpu.SemaphoreType.DMA((16,))],
        compiler_params=pltpu.CompilerParams(vmem_limit_bytes=2**20),
        name="sort_near",
    )(*near_a, *near_b)


KIDS = 8


def early_kernel(fp, fi, sp, si, fu, fut, fw, su, sut, sw):
    @pl.when(pl.program_id(0) == 0)
    def _():
        inv = fi[0]
        pan = fp[0].reshape(PS * B, B)
        fu[...] = mm(pan, inv).astype(BF)
        fut[...] = mm_tt(inv, pan).astype(BF)
        fw[...] = mm_tn(inv, inv)

    for c in range(KIDS):
        inv = si[c]
        pan = sp[c].reshape((Q + 1) * B, B)
        su[c] = mm(pan, inv).astype(BF)
        sut[c] = mm_tt(inv, pan).astype(BF)
        sw[c] = mm_tn(inv, inv)


def early(fp, fi, sp, si):
    n = sp.shape[0]
    whole = lambda *s: pl.BlockSpec(s, lambda i: (0,) * len(s))
    part = lambda *s: pl.BlockSpec((KIDS,) + s, lambda i: (i,) + (0,) * len(s))
    return pl.pallas_call(
        early_kernel,
        grid=(n // KIDS,),
        out_shape=(
            jax.ShapeDtypeStruct((PS * B, B), BF),
            jax.ShapeDtypeStruct((B, PS * B), BF),
            jax.ShapeDtypeStruct((B, B), F32),
            jax.ShapeDtypeStruct((n, (Q + 1) * B, B), BF),
            jax.ShapeDtypeStruct((n, B, (Q + 1) * B), BF),
            jax.ShapeDtypeStruct((n, B, B), F32),
        ),
        in_specs=[
            whole(1, PS, B, B),
            whole(1, B, B),
            part(Q + 1, B, B),
            part(B, B),
        ],
        out_specs=(
            whole(PS * B, B),
            whole(B, PS * B),
            whole(B, B),
            part((Q + 1) * B, B),
            part(B, (Q + 1) * B),
            part(B, B),
        ),
        cost_estimate=pl.CostEstimate(
            flops=300 * 2 * B**3, bytes_accessed=20 * 2**20, transcendentals=0
        ),
        compiler_params=pltpu.CompilerParams(vmem_limit_bytes=58 * 2**20),
        name="early",
    )(fp, fi, sp, si)


def late_kernel(
    pos, fidx, spos,
    a0, a1, a2, a3, b0, b1, b2, b3, fu, fut, fw, su, sut, sw,
    fc_o, fd_o, sc_o, sd_o, cov_o,
    full, tmat, landed, sems,
):
    step = pl.program_id(0)

    @pl.when(step == 0)
    def _():
        me = pos[0]
        row, zh, x = me // 8, (me // 4) % 2, me % 4
        copies = [
            pltpu.make_async_copy(ref, landed.at[n], sems.at[n])
            for n, ref in enumerate((a0, a1, a2, a3, b0, b1, b2, b3))
        ]
        for copy in copies:
            copy.start()
        for half in range(2):
            for t in range(4):
                group = half * 4 + t
                copies[group].wait()
                for u in range(4):
                    dr, dx = (REL[t], REL[u]) if half == 0 else (REL[u], REL[t])
                    r = lax.rem(row - dr + 4, 4)
                    xx = lax.rem(x - dx + 4, 4)
                    for z in range(2):
                        src = r * 8 + lax.rem(zh + z, 2) * 4 + xx
                        first = (3 * src) // 8
                        at = pl.multiple_of(src * SHARD, 16)
                        for k in range(4):
                            col = lax.rem(first + half * 4 + k, NA)
                            full[pl.ds(at, SHARD), pl.ds(pl.multiple_of(col * B, B), B)] = (
                                landed[group, u, z, k * SHARD:(k + 1) * SHARD]
                            )

        def block(p, q):
            return full[
                pl.ds(pl.multiple_of(p * B, B), B), pl.ds(pl.multiple_of(q * B, B), B)
            ]

        for p in range(PS):
            ap = fidx[0, p]
            tmat[(1 + p) * B:(2 + p) * B, (1 + p) * B:(2 + p) * B] = block(ap, ap)
            for q in range(p + 1, PS):
                aq = fidx[0, q]
                near = aq - ap <= 6
                i, j = jnp.where(near, p, q), jnp.where(near, q, p)
                held = block(jnp.where(near, ap, aq), jnp.where(near, aq, ap))
                ri = pl.ds(pl.multiple_of((1 + i) * B, B), B)
                rj = pl.ds(pl.multiple_of((1 + j) * B, B), B)
                tmat[ri, rj] = held
                tmat[rj, ri] = flip(held)
        cross = (-mm(tmat[B:, B:], fu[...])).astype(BF)
        fc_o[...] = cross.reshape(1, PS, B, B)
        tmat[B:, :B] = cross
        for p in range(PS):
            tmat[:B, (1 + p) * B:(2 + p) * B] = flip(cross[p * B:(p + 1) * B])
        diag = (fw[...] - mm(fut[...], cross)).astype(BF)
        fd_o[0] = diag
        tmat[:B, :B] = diag

    for c in range(KIDS):
        kid = step * KIDS + c
        at = [0] + [(1 + spos[kid * Q + q]) * B for q in range(Q)]
        at = [pl.ds(pl.multiple_of(v, B), B) for v in at]
        for r in range(Q + 1):
            line = jnp.concatenate([tmat[at[r], at[q]] for q in range(Q + 1)], axis=1)
            sc_o[c, r] = (-mm(line, su[c])).astype(BF)
    for c in range(KIDS):
        w = sc_o[c].reshape((Q + 1) * B, B)
        d = (sw[c] - mm(sut[c], w)).astype(BF)
        sd_o[c] = d
        cov_o[pl.ds(c * 2 * B, B, stride=2), :] = d.astype(F32)
        cov_o[pl.ds(c * 2 * B + 1, B, stride=2), :] = w[:B].astype(F32)


def final_kernel(
    pos, order, a0, a1, a2, a3, b0, b1, b2, b3, cov_in, rows_o, cov, even, odd, landed, sems
):
    me = pos[0]
    whole = pltpu.make_async_copy(cov_in, cov, sems.at[8])
    whole.start()
    copies = [
        pltpu.make_async_copy(ref, landed.at[n], sems.at[n])
        for n, ref in enumerate((a0, a1, a2, a3, b0, b1, b2, b3))
    ]
    for copy in copies:
        copy.start()
    whole.wait()

    def place(diff):
        diff = lax.rem(diff + 4, 4)
        return jnp.where(diff < 2, diff, 5 - diff)

    def move(t, got):
        for m in range(B):
            src = order[t * B + m]
            got[2 * m:2 * m + 2, :] = cov[pl.ds(pl.multiple_of(src * 2, 2), 2), :]

    def product(t, got):
        line = jnp.concatenate(
            [got[pl.ds(0, B, stride=2), :], got[pl.ds(1, B, stride=2), :]], axis=1
        ).astype(BF)
        by_row = place(me // 8 - t // 8)
        by_x = place(me % 4 - t % 4)
        z = lax.rem((me // 4) % 2 + (t // 4) % 2, 2)
        sens = jnp.concatenate([landed[by_row, by_x, z], landed[4 + by_x, by_row, z]], axis=0)
        rows_o[pl.ds(pl.multiple_of(t * B, B), B)] = mm(line, sens).astype(BF)

    move(0, even)
    for copy in copies:
        copy.wait()

    def pair(i, carry):
        move(2 * i + 1, odd)
        product(2 * i, even)
        move(jnp.minimum(2 * i + 2, TILES - 1), even)
        product(2 * i + 1, odd)
        return carry

    lax.fori_loop(0, TILES // 2, pair, 0)


def final(me, order, ta, tb, cov):
    smem = pl.BlockSpec(memory_space=pltpu.SMEM)
    n = cov.shape[0]
    return pl.pallas_call(
        final_kernel,
        out_shape=jax.ShapeDtypeStruct((n // 2, B), BF),
        in_specs=[smem] * 2 + [pl.BlockSpec(memory_space=pl.ANY)] * 9,
        out_specs=pl.BlockSpec(memory_space=pltpu.VMEM),
        scratch_shapes=[
            pltpu.VMEM((n, B), F32),
            pltpu.VMEM((2 * B, B), F32),
            pltpu.VMEM((2 * B, B), F32),
            pltpu.VMEM((8, 4, 2, B, B), BF),
            pltpu.SemaphoreType.DMA((9,)),
        ],
        cost_estimate=pl.CostEstimate(
            flops=64 * 2 * B**3, bytes_accessed=12 * 2**20, transcendentals=0
        ),
        compiler_params=pltpu.CompilerParams(vmem_limit_bytes=58 * 2**20),
        name="final",
    )(me.reshape(1), order, *ta, *tb, cov)


def late(me, fidx, spos, ga, gb, fu, fut, fw, su, sut, sw):
    n = su.shape[0]
    steps = n // KIDS
    whole = lambda *s: pl.BlockSpec(s, lambda i: (0,) * len(s))
    part = lambda *s: pl.BlockSpec(
        (KIDS,) + s, lambda i: (i,) + (0,) * len(s)
    )
    smem = pl.BlockSpec(memory_space=pltpu.SMEM)
    return pl.pallas_call(
        late_kernel,
        grid=(steps,),
        out_shape=(
            jax.ShapeDtypeStruct((1, PS, B, B), BF),
            jax.ShapeDtypeStruct((1, B, B), BF),
            jax.ShapeDtypeStruct((n, Q + 1, B, B), BF),
            jax.ShapeDtypeStruct((n, B, B), BF),
            jax.ShapeDtypeStruct((2 * n * B, B), F32),
        ),
        in_specs=[smem] * 3
        + [pl.BlockSpec(memory_space=pl.ANY)] * 8
        + [
            whole(PS * B, B),
            whole(B, PS * B),
            whole(B, B),
            part((Q + 1) * B, B),
            part(B, (Q + 1) * B),
            part(B, B),
        ],
        out_specs=(
            whole(1, PS, B, B),
            whole(1, B, B),
            part(Q + 1, B, B),
            part(B, B),
            pl.BlockSpec((2 * KIDS * B, B), lambda i: (i, 0)),
        ),
        scratch_shapes=[
            pltpu.VMEM((NA * B, NA * B), BF),
            pltpu.VMEM(((PS + 1) * B, (PS + 1) * B), BF),
            pltpu.VMEM((8, 4, 2, PART, B), BF),
            pltpu.SemaphoreType.DMA((8,)),
        ],
        cost_estimate=pl.CostEstimate(
            flops=720 * 2 * B**3, bytes_accessed=32 * 2**20, transcendentals=0
        ),
        compiler_params=pltpu.CompilerParams(vmem_limit_bytes=56 * 2**20),
        name="late",
    )(me.reshape(1), fidx, spos.reshape(-1), *ga, *gb, fu, fut, fw, su, sut, sw)


def along_x(v, k):
    return lax.ppermute(
        v, "col", [(z * 4 + x, z * 4 + (x + k) % 4) for z in range(2) for x in range(4)]
    )


def along_row(v, k):
    return lax.ppermute(v, "row", [(r, (r + k) % 4) for r in range(4)])


def spread(v, move):
    return [v] + [move(v, k) for k in REL[1:]]


def local(
    top_covariance,
    first_panel,
    first_inverse,
    first_index,
    second_panel,
    second_inverse,
    second_positions,
    row_order,
    sensitivity,
):
    me = (lax.axis_index("row") * 8 + lax.axis_index("col")).astype(jnp.int32)
    fixed = lax.optimization_barrier
    mine = pack(top_covariance, sensitivity, me)
    other = lax.ppermute(mine, "col", [(c, (c + 4) % 8) for c in range(8)])
    other, *ready = fixed(
        (other, *early(first_panel, first_inverse, second_panel, second_inverse))
    )
    half_a, half_b = fixed((jnp.stack([mine[0], other[0]]), jnp.stack([mine[1], other[1]])))
    near_a, near_b = fixed((spread(half_a, along_x), spread(half_b, along_row)))
    near_a, near_b, sens_a, sens_b = sort_near(near_a, near_b)
    ga, gb = spread(near_a, along_row), spread(near_b, along_x)
    sens_a, sens_b, ga = fixed((sens_a, sens_b, ga))
    ta, tb = spread(sens_a, along_row), spread(sens_b, along_x)
    first_cross, first_diag, second_cross, second_diag, cov = late(
        me, first_index, second_positions, ga, gb, *ready
    )
    products = final(me, row_order, ta, tb, cov)
    tile_products = lax.all_to_all(
        products, ("row", "col"), split_axis=0, concat_axis=0, tiled=True
    )
    return (first_cross, first_diag, second_cross, second_diag, tile_products)


def solution(mesh):
    own = ("grp", "row", "col")
    return jax.shard_map(
        local,
        mesh=mesh,
        in_specs=(
            P(own, None),
            P(own, None, None, None),
            P(own, None, None),
            P(own, None),
            P(own, None, None, None),
            P(own, None, None),
            P(own, None),
            P(own),
            P(own, None, None),
        ),
        out_specs=(
            P(own, None, None, None),
            P(own, None, None),
            P(own, None, None, None),
            P(own, None, None),
            P(own, None),
        ),
        check_vma=False,
    )
```

```python
import jax
import jax.numpy as jnp
from jax import lax
from jax.experimental import pallas as pl
from jax.experimental.pallas import tpu as pltpu
from jax.sharding import PartitionSpec as P

B = 128
NA = 12
PS = 8
Q = 3
WIN = 8
SHARD = 48
PART = 4 * SHARD
SENT = PART + B
TILES = 32
F32 = jnp.float32
BF = jnp.bfloat16
REL = (0, 1, -1, 2)


def mm(a, b):
    return jnp.dot(a, b, preferred_element_type=F32)


def mm_tn(a, b):
    return lax.dot_general(a, b, (((0,), (0,)), ((), ())), preferred_element_type=F32)


def mm_tt(a, b):
    return lax.dot_general(a, b, (((0,), (1,)), ((), ())), preferred_element_type=F32)


def flip(x):
    return x.astype(F32).T.astype(BF)


def pack_kernel(pos, x_ref, s_ref, o_ref):
    first = (3 * pos[0]) // 8
    for k in range(WIN):
        col = lax.rem(first + k, NA)
        at = (k % 4) * SHARD
        o_ref[k // 4, at:at + SHARD] = x_ref[:, pl.ds(pl.multiple_of(col * B, B), B)]
    for h in range(2):
        o_ref[h, 4 * SHARD:] = s_ref[0, h * B:(h + 1) * B]


def pack(x, sens, me):
    return pl.pallas_call(
        pack_kernel,
        out_shape=jax.ShapeDtypeStruct((2, SENT, B), BF),
        in_specs=[
            pl.BlockSpec(memory_space=pltpu.SMEM),
            pl.BlockSpec(memory_space=pltpu.VMEM),
            pl.BlockSpec(memory_space=pltpu.VMEM),
        ],
        out_specs=pl.BlockSpec(memory_space=pltpu.VMEM),
        name="pack",
    )(me.reshape(1), x, sens)


def sort_near_kernel(*refs):
    parts, outs, sems = refs[:8], refs[8:13], refs[13]
    copies = []
    for n, ref in enumerate(parts):
        half, t = n // 4, n % 4
        copies += [
            pltpu.make_async_copy(ref.at[:, pl.ds(0, PART)], outs[half].at[t], sems.at[n]),
            pltpu.make_async_copy(ref.at[:, pl.ds(PART, B)], outs[2 + half].at[t], sems.at[8 + n]),
        ]
        if half == 0:
            copies.append(pltpu.make_async_copy(ref, outs[4].at[t], sems.at[16 + t]))
    for copy in copies:
        copy.start()
    for copy in copies:
        copy.wait()


def sort_near(near_a, near_b):
    any_ = pl.BlockSpec(memory_space=pl.ANY)
    return pl.pallas_call(
        sort_near_kernel,
        out_shape=[jax.ShapeDtypeStruct((4, 2, n, B), BF) for n in (PART, PART, B, B, SENT)],
        in_specs=[any_] * 8,
        out_specs=[any_] * 5,
        scratch_shapes=[pltpu.SemaphoreType.DMA((20,))],
        compiler_params=pltpu.CompilerParams(vmem_limit_bytes=2**20),
        name="sort_near",
    )(*near_a, *near_b)


KIDS = 8


def early_kernel(fp, fi, sp, si, fu, fut, fw, su, sut, sw):
    @pl.when(pl.program_id(0) == 0)
    def _():
        inv = fi[0]
        pan = fp[0].reshape(PS * B, B)
        fu[...] = mm(pan, inv).astype(BF)
        fut[...] = mm_tt(inv, pan).astype(BF)
        fw[...] = mm_tn(inv, inv)

    for c in range(KIDS):
        inv = si[c]
        pan = sp[c].reshape((Q + 1) * B, B)
        su[c] = mm(pan, inv).astype(BF)
        sut[c] = mm_tt(inv, pan).astype(BF)
        sw[c] = mm_tn(inv, inv)


def early(fp, fi, sp, si):
    n = sp.shape[0]
    whole = lambda *s: pl.BlockSpec(s, lambda i: (0,) * len(s))
    part = lambda *s: pl.BlockSpec((KIDS,) + s, lambda i: (i,) + (0,) * len(s))
    return pl.pallas_call(
        early_kernel,
        grid=(n // KIDS,),
        out_shape=(
            jax.ShapeDtypeStruct((PS * B, B), BF),
            jax.ShapeDtypeStruct((B, PS * B), BF),
            jax.ShapeDtypeStruct((B, B), F32),
            jax.ShapeDtypeStruct((n, (Q + 1) * B, B), BF),
            jax.ShapeDtypeStruct((n, B, (Q + 1) * B), BF),
            jax.ShapeDtypeStruct((n, B, B), F32),
        ),
        in_specs=[
            whole(1, PS, B, B),
            whole(1, B, B),
            part(Q + 1, B, B),
            part(B, B),
        ],
        out_specs=(
            whole(PS * B, B),
            whole(B, PS * B),
            whole(B, B),
            part((Q + 1) * B, B),
            part(B, (Q + 1) * B),
            part(B, B),
        ),
        cost_estimate=pl.CostEstimate(
            flops=300 * 2 * B**3, bytes_accessed=20 * 2**20, transcendentals=0
        ),
        compiler_params=pltpu.CompilerParams(vmem_limit_bytes=58 * 2**20),
        name="early",
    )(fp, fi, sp, si)


def late_kernel(
    pos, fidx, spos,
    a0, a1, a2, a3, b0, b1, b2, b3, fu, fut, fw, su, sut, sw,
    fc_o, fd_o, sc_o, sd_o, cov_o,
    full, tmat, landed, sems,
):
    step = pl.program_id(0)

    @pl.when(step == 0)
    def _():
        me = pos[0]
        row, zh, x = me // 8, (me // 4) % 2, me % 4
        copies = [
            pltpu.make_async_copy(
                ref.at[:, :, pl.ds(0, PART)] if n == 3 else ref, landed.at[n], sems.at[n]
            )
            for n, ref in enumerate((a0, a1, a2, a3, b0, b1, b2, b3))
        ]
        for copy in copies:
            copy.start()
        for half in range(2):
            for t in range(4):
                group = half * 4 + t
                copies[group].wait()
                for u in range(4):
                    dr, dx = (REL[t], REL[u]) if half == 0 else (REL[u], REL[t])
                    r = lax.rem(row - dr + 4, 4)
                    xx = lax.rem(x - dx + 4, 4)
                    for z in range(2):
                        src = r * 8 + lax.rem(zh + z, 2) * 4 + xx
                        first = (3 * src) // 8
                        at = pl.multiple_of(src * SHARD, 16)
                        for k in range(4):
                            col = lax.rem(first + half * 4 + k, NA)
                            full[pl.ds(at, SHARD), pl.ds(pl.multiple_of(col * B, B), B)] = (
                                landed[group, u, z, k * SHARD:(k + 1) * SHARD]
                            )

        def block(p, q):
            return full[
                pl.ds(pl.multiple_of(p * B, B), B), pl.ds(pl.multiple_of(q * B, B), B)
            ]

        for p in range(PS):
            ap = fidx[0, p]
            tmat[(1 + p) * B:(2 + p) * B, (1 + p) * B:(2 + p) * B] = block(ap, ap)
            for q in range(p + 1, PS):
                aq = fidx[0, q]
                near = aq - ap <= 6
                i, j = jnp.where(near, p, q), jnp.where(near, q, p)
                held = block(jnp.where(near, ap, aq), jnp.where(near, aq, ap))
                ri = pl.ds(pl.multiple_of((1 + i) * B, B), B)
                rj = pl.ds(pl.multiple_of((1 + j) * B, B), B)
                tmat[ri, rj] = held
                tmat[rj, ri] = flip(held)
        cross = (-mm(tmat[B:, B:], fu[...])).astype(BF)
        fc_o[...] = cross.reshape(1, PS, B, B)
        tmat[B:, :B] = cross
        for p in range(PS):
            tmat[:B, (1 + p) * B:(2 + p) * B] = flip(cross[p * B:(p + 1) * B])
        diag = (fw[...] - mm(fut[...], cross)).astype(BF)
        fd_o[0] = diag
        tmat[:B, :B] = diag

    for c in range(KIDS):
        kid = step * KIDS + c
        at = [0] + [(1 + spos[kid * Q + q]) * B for q in range(Q)]
        at = [pl.ds(pl.multiple_of(v, B), B) for v in at]
        for r in range(Q + 1):
            line = jnp.concatenate([tmat[at[r], at[q]] for q in range(Q + 1)], axis=1)
            sc_o[c, r] = (-mm(line, su[c])).astype(BF)
    for c in range(KIDS):
        w = sc_o[c].reshape((Q + 1) * B, B)
        d = (sw[c] - mm(sut[c], w)).astype(BF)
        sd_o[c] = d
        cov_o[pl.ds(c * 2 * B, B, stride=2), :] = d.astype(F32)
        cov_o[pl.ds(c * 2 * B + 1, B, stride=2), :] = w[:B].astype(F32)


def final_kernel(
    pos, order, a0, a1, a2, a3, b0, b1, b2, b3, cov_in, rows_o, cov, even, odd, landed, sems
):
    me = pos[0]
    whole = pltpu.make_async_copy(cov_in, cov, sems.at[8])
    whole.start()
    copies = [
        pltpu.make_async_copy(
            ref.at[:, :, pl.ds(PART, B)] if n == 3 else ref, landed.at[n], sems.at[n]
        )
        for n, ref in enumerate((a0, a1, a2, a3, b0, b1, b2, b3))
    ]
    for copy in copies:
        copy.start()
    whole.wait()

    def place(diff):
        diff = lax.rem(diff + 4, 4)
        return jnp.where(diff < 2, diff, 5 - diff)

    def move(t, got):
        for m in range(B):
            src = order[t * B + m]
            got[2 * m:2 * m + 2, :] = cov[pl.ds(pl.multiple_of(src * 2, 2), 2), :]

    def product(t, got):
        line = jnp.concatenate(
            [got[pl.ds(0, B, stride=2), :], got[pl.ds(1, B, stride=2), :]], axis=1
        ).astype(BF)
        by_row = place(me // 8 - t // 8)
        by_x = place(me % 4 - t % 4)
        z = lax.rem((me // 4) % 2 + (t // 4) % 2, 2)
        sens = jnp.concatenate([landed[by_row, by_x, z], landed[4 + by_x, by_row, z]], axis=0)
        rows_o[pl.ds(pl.multiple_of(t * B, B), B)] = mm(line, sens).astype(BF)

    move(0, even)
    for copy in copies:
        copy.wait()

    def pair(i, carry):
        move(2 * i + 1, odd)
        product(2 * i, even)
        move(jnp.minimum(2 * i + 2, TILES - 1), even)
        product(2 * i + 1, odd)
        return carry

    lax.fori_loop(0, TILES // 2, pair, 0)


def final(me, order, ta, tb, cov):
    smem = pl.BlockSpec(memory_space=pltpu.SMEM)
    n = cov.shape[0]
    return pl.pallas_call(
        final_kernel,
        out_shape=jax.ShapeDtypeStruct((n // 2, B), BF),
        in_specs=[smem] * 2 + [pl.BlockSpec(memory_space=pl.ANY)] * 9,
        out_specs=pl.BlockSpec(memory_space=pltpu.VMEM),
        scratch_shapes=[
            pltpu.VMEM((n, B), F32),
            pltpu.VMEM((2 * B, B), F32),
            pltpu.VMEM((2 * B, B), F32),
            pltpu.VMEM((8, 4, 2, B, B), BF),
            pltpu.SemaphoreType.DMA((9,)),
        ],
        cost_estimate=pl.CostEstimate(
            flops=64 * 2 * B**3, bytes_accessed=12 * 2**20, transcendentals=0
        ),
        compiler_params=pltpu.CompilerParams(vmem_limit_bytes=58 * 2**20),
        name="final",
    )(me.reshape(1), order, *ta, *tb, cov)


def late(me, fidx, spos, ga, gb, fu, fut, fw, su, sut, sw):
    n = su.shape[0]
    steps = n // KIDS
    whole = lambda *s: pl.BlockSpec(s, lambda i: (0,) * len(s))
    part = lambda *s: pl.BlockSpec(
        (KIDS,) + s, lambda i: (i,) + (0,) * len(s)
    )
    smem = pl.BlockSpec(memory_space=pltpu.SMEM)
    return pl.pallas_call(
        late_kernel,
        grid=(steps,),
        out_shape=(
            jax.ShapeDtypeStruct((1, PS, B, B), BF),
            jax.ShapeDtypeStruct((1, B, B), BF),
            jax.ShapeDtypeStruct((n, Q + 1, B, B), BF),
            jax.ShapeDtypeStruct((n, B, B), BF),
            jax.ShapeDtypeStruct((2 * n * B, B), F32),
        ),
        in_specs=[smem] * 3
        + [pl.BlockSpec(memory_space=pl.ANY)] * 8
        + [
            whole(PS * B, B),
            whole(B, PS * B),
            whole(B, B),
            part((Q + 1) * B, B),
            part(B, (Q + 1) * B),
            part(B, B),
        ],
        out_specs=(
            whole(1, PS, B, B),
            whole(1, B, B),
            part(Q + 1, B, B),
            part(B, B),
            pl.BlockSpec((2 * KIDS * B, B), lambda i: (i, 0)),
        ),
        scratch_shapes=[
            pltpu.VMEM((NA * B, NA * B), BF),
            pltpu.VMEM(((PS + 1) * B, (PS + 1) * B), BF),
            pltpu.VMEM((8, 4, 2, PART, B), BF),
            pltpu.SemaphoreType.DMA((8,)),
        ],
        cost_estimate=pl.CostEstimate(
            flops=720 * 2 * B**3, bytes_accessed=32 * 2**20, transcendentals=0
        ),
        compiler_params=pltpu.CompilerParams(vmem_limit_bytes=56 * 2**20),
        name="late",
    )(me.reshape(1), fidx, spos.reshape(-1), *ga, *gb, fu, fut, fw, su, sut, sw)


def along_x(v, k):
    return lax.ppermute(
        v, "col", [(z * 4 + x, z * 4 + (x + k) % 4) for z in range(2) for x in range(4)]
    )


def along_row(v, k):
    return lax.ppermute(v, "row", [(r, (r + k) % 4) for r in range(4)])


def spread(v, move):
    return [v] + [move(v, k) for k in REL[1:]]


def local(
    top_covariance,
    first_panel,
    first_inverse,
    first_index,
    second_panel,
    second_inverse,
    second_positions,
    row_order,
    sensitivity,
):
    me = (lax.axis_index("row") * 8 + lax.axis_index("col")).astype(jnp.int32)
    fixed = lax.optimization_barrier
    mine = pack(top_covariance, sensitivity, me)
    other = lax.ppermute(mine, "col", [(c, (c + 4) % 8) for c in range(8)])
    other, *ready = fixed(
        (other, *early(first_panel, first_inverse, second_panel, second_inverse))
    )
    half_a, half_b = fixed((jnp.stack([mine[0], other[0]]), jnp.stack([mine[1], other[1]])))
    near_a, near_b = fixed((spread(half_a, along_x), spread(half_b, along_row)))
    near_a, near_b, sens_a, sens_b, both_a = sort_near(near_a, near_b)
    ga = [near_a, along_row(near_a, 1), along_row(near_a, -1), along_row(both_a, 2)]
    gb = spread(near_b, along_x)
    sens_a, sens_b, ga = fixed((sens_a, sens_b, ga))
    ta = [sens_a, along_row(sens_a, 1), along_row(sens_a, -1), ga[3]]
    tb = spread(sens_b, along_x)
    first_cross, first_diag, second_cross, second_diag, cov = late(
        me, first_index, second_positions, ga, gb, *ready
    )
    products = final(me, row_order, ta, tb, cov)
    tile_products = lax.all_to_all(
        products, ("row", "col"), split_axis=0, concat_axis=0, tiled=True
    )
    return (first_cross, first_diag, second_cross, second_diag, tile_products)


def solution(mesh):
    own = ("grp", "row", "col")
    return jax.shard_map(
        local,
        mesh=mesh,
        in_specs=(
            P(own, None),
            P(own, None, None, None),
            P(own, None, None),
            P(own, None),
            P(own, None, None, None),
            P(own, None, None),
            P(own, None),
            P(own),
            P(own, None, None),
        ),
        out_specs=(
            P(own, None, None, None),
            P(own, None, None),
            P(own, None, None, None),
            P(own, None, None),
            P(own, None),
        ),
        check_vma=False,
    )
```

```python
import functools

import jax
import jax.numpy as jnp
from jax import lax
from jax.experimental import pallas as pl
from jax.experimental.pallas import tpu as pltpu
from jax.sharding import PartitionSpec as P

B = 128
NA = 12
PS = 8
Q = 3
WIN = 8
SHARD = 48
SENT = 4 * SHARD + B
TILES = 32
F32 = jnp.float32
BF = jnp.bfloat16
REL = (0, 1, -1, 2)


def mm(a, b):
    return jnp.dot(a, b, preferred_element_type=F32)


def mm_tn(a, b):
    return lax.dot_general(a, b, (((0,), (0,)), ((), ())), preferred_element_type=F32)


def mm_tt(a, b):
    return lax.dot_general(a, b, (((0,), (1,)), ((), ())), preferred_element_type=F32)


def flip(x):
    return x.astype(F32).T.astype(BF)


def pack_kernel(pos, x_ref, s_ref, o_ref):
    first = (3 * pos[0]) // 8
    for k in range(WIN):
        col = lax.rem(first + k, NA)
        at = (k % 4) * SHARD
        o_ref[k // 4, at:at + SHARD] = x_ref[:, pl.ds(pl.multiple_of(col * B, B), B)]
    for h in range(2):
        o_ref[h, 4 * SHARD:] = s_ref[0, h * B:(h + 1) * B]


def pack(x, sens, me):
    return pl.pallas_call(
        pack_kernel,
        out_shape=jax.ShapeDtypeStruct((2, SENT, B), BF),
        in_specs=[
            pl.BlockSpec(memory_space=pltpu.SMEM),
            pl.BlockSpec(memory_space=pltpu.VMEM),
            pl.BlockSpec(memory_space=pltpu.VMEM),
        ],
        out_specs=pl.BlockSpec(memory_space=pltpu.VMEM),
        name="pack",
    )(me.reshape(1), x, sens)


KIDS = 16


def early_kernel(fp, fi, sp, si, fu, fut, fw, su, sut, sw):
    @pl.when(pl.program_id(0) == 0)
    def _():
        inv = fi[0]
        pan = fp[0].reshape(PS * B, B)
        fu[...] = mm(pan, inv).astype(BF)
        fut[...] = mm_tt(inv, pan).astype(BF)
        fw[...] = mm_tn(inv, inv)

    for c in range(KIDS):
        inv = si[c]
        pan = sp[c].reshape((Q + 1) * B, B)
        su[c] = mm(pan, inv).astype(BF)
        sut[c] = mm_tt(inv, pan).astype(BF)
        sw[c] = mm_tn(inv, inv)


def early(fp, fi, sp, si):
    n = sp.shape[0]
    whole = lambda *s: pl.BlockSpec(s, lambda i: (0,) * len(s))
    part = lambda *s: pl.BlockSpec((KIDS,) + s, lambda i: (i,) + (0,) * len(s))
    return pl.pallas_call(
        early_kernel,
        grid=(n // KIDS,),
        out_shape=(
            jax.ShapeDtypeStruct((PS * B, B), BF),
            jax.ShapeDtypeStruct((B, PS * B), BF),
            jax.ShapeDtypeStruct((B, B), F32),
            jax.ShapeDtypeStruct((n, (Q + 1) * B, B), BF),
            jax.ShapeDtypeStruct((n, B, (Q + 1) * B), BF),
            jax.ShapeDtypeStruct((n, B, B), F32),
        ),
        in_specs=[
            whole(1, PS, B, B),
            whole(1, B, B),
            part(Q + 1, B, B),
            part(B, B),
        ],
        out_specs=(
            whole(PS * B, B),
            whole(B, PS * B),
            whole(B, B),
            part((Q + 1) * B, B),
            part(B, (Q + 1) * B),
            part(B, B),
        ),
        cost_estimate=pl.CostEstimate(
            flops=300 * 2 * B**3, bytes_accessed=20 * 2**20, transcendentals=0
        ),
        compiler_params=pltpu.CompilerParams(vmem_limit_bytes=20 * 2**20),
        name="early",
    )(fp, fi, sp, si)


def late_kernel(
    steps, pos, fidx, spos, order,
    a0, a1, a2, a3, b0, b1, b2, b3, fu, fut, fw, su, sut, sw,
    fc_o, fd_o, sc_o, sd_o, rows_o,
    full, tmat, cov, even, odd, sens, landed, sems,
):
    step = pl.program_id(0)

    @pl.when(step == 0)
    def _():
        me = pos[0]
        row, zh, x = me // 8, (me // 4) % 2, me % 4
        copies = [
            pltpu.make_async_copy(ref, landed.at[n], sems.at[n])
            for n, ref in enumerate((a0, a1, a2, a3, b0, b1, b2, b3))
        ]
        for copy in copies:
            copy.start()
        for half in range(2):
            for t in range(4):
                group = half * 4 + t
                copies[group].wait()
                for u in range(4):
                    dr, dx = (REL[t], REL[u]) if half == 0 else (REL[u], REL[t])
                    r = lax.rem(row - dr + 4, 4)
                    xx = lax.rem(x - dx + 4, 4)
                    for z in range(2):
                        src = r * 8 + lax.rem(zh + z, 2) * 4 + xx
                        first = (3 * src) // 8
                        at = pl.multiple_of(src * SHARD, 16)
                        for k in range(4):
                            col = lax.rem(first + half * 4 + k, NA)
                            full[pl.ds(at, SHARD), pl.ds(pl.multiple_of(col * B, B), B)] = (
                                landed[group, u, z, k * SHARD:(k + 1) * SHARD]
                            )
                        sens[src, half * B:(half + 1) * B] = landed[group, u, z, 4 * SHARD:]

        def block(p, q):
            return full[
                pl.ds(pl.multiple_of(p * B, B), B), pl.ds(pl.multiple_of(q * B, B), B)
            ]

        for p in range(PS):
            ap = fidx[0, p]
            tmat[(1 + p) * B:(2 + p) * B, (1 + p) * B:(2 + p) * B] = block(ap, ap)
            for q in range(p + 1, PS):
                aq = fidx[0, q]
                near = aq - ap <= 6
                i, j = jnp.where(near, p, q), jnp.where(near, q, p)
                held = block(jnp.where(near, ap, aq), jnp.where(near, aq, ap))
                ri = pl.ds(pl.multiple_of((1 + i) * B, B), B)
                rj = pl.ds(pl.multiple_of((1 + j) * B, B), B)
                tmat[ri, rj] = held
                tmat[rj, ri] = flip(held)
        cross = (-mm(tmat[B:, B:], fu[...])).astype(BF)
        fc_o[...] = cross.reshape(1, PS, B, B)
        tmat[B:, :B] = cross
        for p in range(PS):
            tmat[:B, (1 + p) * B:(2 + p) * B] = flip(cross[p * B:(p + 1) * B])
        diag = (fw[...] - mm(fut[...], cross)).astype(BF)
        fd_o[0] = diag
        tmat[:B, :B] = diag

    @pl.when(step < steps)
    def _():
        for c in range(KIDS):
            kid = step * KIDS + c
            at = [0] + [(1 + spos[kid * Q + q]) * B for q in range(Q)]
            at = [pl.ds(pl.multiple_of(v, B), B) for v in at]
            for r in range(Q + 1):
                line = jnp.concatenate([tmat[at[r], at[q]] for q in range(Q + 1)], axis=1)
                sc_o[c, r] = (-mm(line, su[c])).astype(BF)
        for c in range(KIDS):
            w = sc_o[c].reshape((Q + 1) * B, B)
            d = (sw[c] - mm(sut[c], w)).astype(BF)
            sd_o[c] = d
            base = pl.multiple_of((step * KIDS + c) * 2 * B, 2 * B)
            cov[pl.ds(base, B, stride=2), :] = d.astype(F32)
            cov[pl.ds(base + 1, B, stride=2), :] = w[:B].astype(F32)

    @pl.when(step == steps)
    def _():
        def move(t, got):
            for m in range(B):
                src = order[t * B + m]
                got[2 * m:2 * m + 2, :] = cov[pl.ds(pl.multiple_of(src * 2, 2), 2), :]

        def product(t, got):
            line = jnp.concatenate(
                [got[pl.ds(0, B, stride=2), :], got[pl.ds(1, B, stride=2), :]], axis=1
            ).astype(BF)
            rows_o[pl.ds(pl.multiple_of(t * B, B), B)] = mm(line, sens[t]).astype(BF)

        move(0, even)

        def pair(i, carry):
            move(2 * i + 1, odd)
            product(2 * i, even)
            move(jnp.minimum(2 * i + 2, TILES - 1), even)
            product(2 * i + 1, odd)
            return carry

        lax.fori_loop(0, TILES // 2, pair, 0)


def late(me, fidx, spos, order, ga, gb, fu, fut, fw, su, sut, sw):
    n = su.shape[0]
    steps = n // KIDS
    whole = lambda *s: pl.BlockSpec(s, lambda i: (0,) * len(s))
    part = lambda *s: pl.BlockSpec(
        (KIDS,) + s, lambda i: (jnp.minimum(i, steps - 1),) + (0,) * len(s)
    )
    smem = pl.BlockSpec(memory_space=pltpu.SMEM)
    return pl.pallas_call(
        functools.partial(late_kernel, steps),
        grid=(steps + 1,),
        out_shape=(
            jax.ShapeDtypeStruct((1, PS, B, B), BF),
            jax.ShapeDtypeStruct((1, B, B), BF),
            jax.ShapeDtypeStruct((n, Q + 1, B, B), BF),
            jax.ShapeDtypeStruct((n, B, B), BF),
            jax.ShapeDtypeStruct((n * B, B), BF),
        ),
        in_specs=[smem] * 4
        + [pl.BlockSpec(memory_space=pl.ANY)] * 8
        + [
            whole(PS * B, B),
            whole(B, PS * B),
            whole(B, B),
            part((Q + 1) * B, B),
            part(B, (Q + 1) * B),
            part(B, B),
        ],
        out_specs=(
            whole(1, PS, B, B),
            whole(1, B, B),
            part(Q + 1, B, B),
            part(B, B),
            whole(n * B, B),
        ),
        scratch_shapes=[
            pltpu.VMEM((NA * B, NA * B), BF),
            pltpu.VMEM(((PS + 1) * B, (PS + 1) * B), BF),
            pltpu.VMEM((2 * n * B, B), F32),
            pltpu.VMEM((2 * B, B), F32),
            pltpu.VMEM((2 * B, B), F32),
            pltpu.VMEM((TILES, 2 * B, B), BF),
            pltpu.VMEM((8, 4, 2, SENT, B), BF),
            pltpu.SemaphoreType.DMA((8,)),
        ],
        cost_estimate=pl.CostEstimate(
            flops=720 * 2 * B**3, bytes_accessed=20 * 2**20, transcendentals=0
        ),
        compiler_params=pltpu.CompilerParams(vmem_limit_bytes=36 * 2**20),
        name="late",
    )(me.reshape(1), fidx, spos.reshape(-1), order, *ga, *gb, fu, fut, fw, su, sut, sw)


def along_x(v, k):
    return lax.ppermute(
        v, "col", [(z * 4 + x, z * 4 + (x + k) % 4) for z in range(2) for x in range(4)]
    )


def along_row(v, k):
    return lax.ppermute(v, "row", [(r, (r + k) % 4) for r in range(4)])


def spread(v, move):
    return [v] + [move(v, k) for k in REL[1:]]


def local(
    top_covariance,
    first_panel,
    first_inverse,
    first_index,
    second_panel,
    second_inverse,
    second_positions,
    row_order,
    sensitivity,
):
    me = (lax.axis_index("row") * 8 + lax.axis_index("col")).astype(jnp.int32)
    fixed = lax.optimization_barrier
    mine = pack(top_covariance, sensitivity, me)
    other = lax.ppermute(mine, "col", [(c, (c + 4) % 8) for c in range(8)])
    half_a, half_b = fixed((jnp.stack([mine[0], other[0]]), jnp.stack([mine[1], other[1]])))
    near_a, near_b = fixed((spread(half_a, along_x), spread(half_b, along_row)))
    near_a, near_b = fixed((jnp.stack(near_a), jnp.stack(near_b)))
    ga, gb = spread(near_a, along_row), spread(near_b, along_x)
    fu, fut, fw, su, sut, sw = early(first_panel, first_inverse, second_panel, second_inverse)
    first_cross, first_diag, second_cross, second_diag, products = late(
        me, first_index, second_positions, row_order, ga, gb, fu, fut, fw, su, sut, sw
    )
    tile_products = lax.all_to_all(
        products, ("row", "col"), split_axis=0, concat_axis=0, tiled=True
    )
    return (first_cross, first_diag, second_cross, second_diag, tile_products)


def solution(mesh):
    own = ("grp", "row", "col")
    return jax.shard_map(
        local,
        mesh=mesh,
        in_specs=(
            P(own, None),
            P(own, None, None, None),
            P(own, None, None),
            P(own, None),
            P(own, None, None, None),
            P(own, None, None),
            P(own, None),
            P(own),
            P(own, None, None),
        ),
        out_specs=(
            P(own, None, None, None),
            P(own, None, None),
            P(own, None, None, None),
            P(own, None, None),
            P(own, None),
        ),
        check_vma=False,
    )
```
